32 devices in a mesh: outer: 4 (over z), inner: 4 (over x, core), head: 2 (over y).
Axes of the slice: x: 2, y: 2, z: 4, core: 2. Of those that a mesh axis runs over, the one named last changes fastest.
Arguments:
- queries: bfloat16 [4096, 4096], P(('outer', 'inner', 'head')), may hold values from -6 to 6
- keys: bfloat16 [4096, 512], P(('outer', 'inner', 'head')), may hold values from -6 to 6
- values: bfloat16 [4096, 512], P(('outer', 'inner', 'head')), may hold values from -6 to 6
- doc_lengths: int32 [256], replicated, may hold values from 1 to 256, 4096 in all
Outputs:
- attended: bfloat16 [4096, 4096], P(('outer', 'inner', 'head'))
The draws below stay inside these ranges and needn't reach their ends.
Inputs may be any that keep to these rules, and one draw needn't show every extreme that they name: `doc_lengths`: the documents lie end to end in order of position; the lengths sum to 4096 and the largest is exactly 256.
All inputs are finite; a program needn't handle non-finite values.
Results may differ from the reference program's by a relative error of at most 0.0019.
Values may be sent and summed in bfloat16 or wider, within the bound.
A program may use at most 64 MiB of HBM per device.

```python
import math
import jax
import jax.numpy as jnp
import numpy as np
from jax import lax

QUERY_HEAD_COUNT = 32
KEY_VALUE_HEADS = 4
HEAD_WIDTH = 128
BLOCK_TOKENS = 128
DOCUMENT_SPAN = 2
QUERY_PER_KEY = 8
SEQUENCE_TOKENS = 4096
MAXDOC = 256
NDOC = 256
N_OUTER = 4
N_INNER = 4


def draw_keys(key, part):
    attention_output = jnp.clip(jax.random.normal(jax.random.fold_in(key, 2), (SEQUENCE_TOKENS, KEY_VALUE_HEADS * HEAD_WIDTH), jnp.float32), -4.0, 4.0)
    return attention_output.astype(jnp.bfloat16)


def draw_queries(key, part):
    attention_output = jnp.clip(jax.random.normal(jax.random.fold_in(key, 1), (SEQUENCE_TOKENS, QUERY_HEAD_COUNT * HEAD_WIDTH), jnp.float32), -4.0, 4.0)
    return attention_output.astype(jnp.bfloat16)


def block_levels(key, extent, split, least, high):
    loudness, own = 1.0, jax.random.fold_in(key, 6)
    for axis_at, shards_of in split:
        heights = jnp.exp(jax.random.uniform(jax.random.fold_in(own, axis_at), (shards_of,), jnp.float32, least / len(split), high / len(split)))
        loudness = loudness * jnp.repeat(heights, extent[axis_at] // shards_of).reshape([-1 if axis == axis_at else 1 for axis in range(len(extent))])
    return loudness


def split_up(count, total, most, skew):
    loads = [(1 << 20) // math.isqrt(standing ** skew) + 1 for standing in range(2, count + 1)]
    surplus, counts = total - most - (count - 1), [1] * (count - 1)
    while surplus > 0:
        movable = [i for i in range(count - 1) if counts[i] < most]
        whole, left = sum([loads[i] for i in movable]), surplus
        for i in movable:
            more = min(most - counts[i], max(1, left * loads[i] // whole), surplus)
            counts[i] = counts[i] + more
            surplus = surplus - more
    return np.array([most] + counts)


def ragged(stream_key, amount, total, most, slope):
    if amount == 2:
        one = jax.random.randint(stream_key, (), max(1, total - most), min(most, total - 1) + 1)
        return jnp.stack([one, total - one])
    sizes = jnp.asarray(split_up(amount, total, most, slope), jnp.int32)
    couples = (amount - 1) // 2
    source_of, receiver = sizes[1:1 + 2 * couples:2], sizes[2:2 + 2 * couples:2]
    margin = jnp.minimum(source_of - 1, most - receiver)
    passed = jax.random.randint(jax.random.fold_in(stream_key, 1), (couples,), 0, 1 << 20) % (margin + 1)
    sizes = sizes.at[1:1 + 2 * couples:2].set(source_of - passed).at[2:2 + 2 * couples:2].set(receiver + passed)
    return sizes[jax.random.permutation(jax.random.fold_in(stream_key, 2), amount)]


def noise(rng, extent, scale, most, split=(), held_as=jnp.bfloat16):
    values = jax.random.normal(rng, extent, jnp.float32) * scale
    if len(split) > 0:
        values = block_levels(rng, extent, split, -0.22, 0.18) * values
    return jnp.clip(values, min=-most, max=most).astype(held_as)


def setup_inputs(seed: int = 0) -> dict:
    seeds = jax.random.split(jax.random.key(seed), 5)
    return {
        "queries": draw_queries(jax.random.fold_in(seeds[4], 71), 0),
        "keys": draw_keys(jax.random.fold_in(seeds[4], 71), 0),
        "values": noise(seeds[2], (SEQUENCE_TOKENS, KEY_VALUE_HEADS * HEAD_WIDTH), 1.0, 6.0, ((0, 32),)),
        "doc_lengths": ragged(seeds[3], NDOC, SEQUENCE_TOKENS, MAXDOC, 2).astype(jnp.int32),
    }


NEG = -1e+30

def sorted_ordering(array, context_block_count):
    halves = array.reshape(context_block_count, 2, BLOCK_TOKENS, array.shape[-1])
    return jnp.concatenate([halves[:, 0], halves[::-1, 1]], axis=0)

def reference(queries, keys, values, doc_lengths):
    context_block_count = N_OUTER * N_INNER
    segment_count = 2 * context_block_count
    query_segments = sorted_ordering(queries, context_block_count).reshape(segment_count, BLOCK_TOKENS, KEY_VALUE_HEADS, QUERY_PER_KEY, HEAD_WIDTH)
    key_stretches = sorted_ordering(keys, context_block_count)
    value_stretches = sorted_ordering(values, context_block_count)
    padding_amount = jnp.zeros((DOCUMENT_SPAN, BLOCK_TOKENS, KEY_VALUE_HEADS * HEAD_WIDTH), keys.dtype)
    key_with_padding = jnp.concatenate([padding_amount, key_stretches], axis=0)
    value_with_padding = jnp.concatenate([padding_amount, value_stretches], axis=0)
    doc_ends = jnp.cumsum(doc_lengths).astype(jnp.int32)
    positions = jnp.arange(SEQUENCE_TOKENS, dtype=jnp.int32)
    doc_ids = jnp.searchsorted(doc_ends, positions, side='right').astype(jnp.int32).reshape(segment_count, BLOCK_TOKENS)
    doc_padded = jnp.concatenate([jnp.full((DOCUMENT_SPAN, BLOCK_TOKENS), -1, jnp.int32), doc_ids], axis=0)
    visible_span = (DOCUMENT_SPAN + 1) * BLOCK_TOKENS
    offsets = jnp.arange(BLOCK_TOKENS, dtype=jnp.int32)
    spread = jnp.arange(visible_span, dtype=jnp.int32)
    score_scale = 1.0 / math.sqrt(HEAD_WIDTH)

    def one_stretch(segment_index):
        query_block = lax.dynamic_index_in_dim(query_segments, segment_index, 0, keepdims=False).astype(jnp.float32)
        key_tile_rows = lax.dynamic_slice_in_dim(key_with_padding, segment_index, DOCUMENT_SPAN + 1, 0).reshape(visible_span, KEY_VALUE_HEADS, HEAD_WIDTH).astype(jnp.float32)
        value_tile_rows = lax.dynamic_slice_in_dim(value_with_padding, segment_index, DOCUMENT_SPAN + 1, 0).reshape(visible_span, KEY_VALUE_HEADS, HEAD_WIDTH).astype(jnp.float32)
        key_docs = lax.dynamic_slice_in_dim(doc_padded, segment_index, DOCUMENT_SPAN + 1, 0).reshape(visible_span)
        query_docs = lax.dynamic_index_in_dim(doc_ids, segment_index, 0, keepdims=False)
        query_positions = segment_index * BLOCK_TOKENS + offsets
        key_positions = (segment_index - DOCUMENT_SPAN) * BLOCK_TOKENS + spread
        allowed = (query_docs[:, None] == key_docs[None, :]) & (key_positions[None, :] <= query_positions[:, None])
        scores = jnp.einsum('qhgd,khd->hgqk', query_block, key_tile_rows) * score_scale
        scores = jnp.where(allowed, scores, NEG)
        maximum = lax.optimization_barrier(jnp.max(scores, axis=-1, keepdims=True))
        weights = jnp.where(allowed, jnp.exp(scores - maximum), 0.0)
        totals = lax.optimization_barrier(jnp.sum(weights, axis=-1))
        rounded = lax.optimization_barrier(weights.astype(jnp.bfloat16)).astype(jnp.float32)
        summed = jnp.einsum('hgqk,khd->hgqd', rounded, value_tile_rows)
        attention_output = (summed / totals[..., None]).transpose(2, 0, 1, 3)
        return attention_output.reshape(BLOCK_TOKENS, QUERY_HEAD_COUNT * HEAD_WIDTH).astype(jnp.bfloat16)
    attended = lax.map(one_stretch, jnp.arange(segment_count, dtype=jnp.int32))
    front = attended[:context_block_count]
    behind = attended[context_block_count:][::-1]
    return jnp.stack([front, behind], axis=1).reshape(SEQUENCE_TOKENS, QUERY_HEAD_COUNT * HEAD_WIDTH)
```

```python
import functools
import math

import jax
import jax.numpy as jnp
from jax import lax
from jax.experimental import pallas as pl
from jax.experimental.pallas import tpu as pltpu
from jax.sharding import PartitionSpec as P

HEAD_WIDTH = 128
DOCUMENT_SPAN = 2
QUERY_PER_KEY = 8
LANES = 128

NEG = -1e30


def piece_to_device(piece, contexts, inner_count, per_block):
    block, sub = piece // per_block, piece % per_block
    front = block < contexts
    context = jnp.where(front, block, 2 * contexts - 1 - block)
    head = jnp.where(front, sub, per_block + sub)
    return (context // inner_count, context % inner_count, head)


def document_starts(lengths, positions):
    lane = lax.broadcasted_iota(jnp.int32, lengths.shape, 1)
    within = lengths
    step = 1
    while step < LANES:
        within = within + jnp.where(lane >= step, pltpu.roll(within, step, 1), 0)
        step *= 2
    before = jnp.zeros((1, 1), jnp.int32)
    starts = jnp.zeros(positions.shape, jnp.int32)
    for row in range(lengths.shape[0]):
        ends = before + within[row : row + 1, :]
        starts = jnp.maximum(starts, jnp.where(ends <= positions, ends, 0))
        before = ends[:, LANES - 1 :]
    return jnp.max(starts, axis=1, keepdims=True)


def kernel(sizes, q_hbm, k_hbm, v_hbm, len_ref, o_hbm, q_buf, k_buf, v_buf, o_buf, bias,
           send_sem, recv_sem, in_sem, out_sem):
    outer_count, inner_count, head_count = sizes
    rows, kv_width = k_hbm.shape
    key_heads = kv_width // HEAD_WIDTH
    contexts = outer_count * inner_count
    per_block = head_count // 2
    reach = DOCUMENT_SPAN * rows * per_block
    hops = reach // rows
    pieces = contexts * head_count
    own_rows = k_buf.shape[0] - reach

    context = lax.axis_index("outer") * inner_count + lax.axis_index("inner")
    head = lax.axis_index("head")
    half, sub = head // per_block, head % per_block
    block = jnp.where(half == 0, context, 2 * contexts - 1 - context)
    piece = block * per_block + sub
    place = functools.partial(
        piece_to_device, contexts=contexts, inner_count=inner_count, per_block=per_block)
    following = place(lax.rem(piece + 1, pieces))
    preceding = place(lax.rem(piece + pieces - 1, pieces))

    barrier = pltpu.get_barrier_semaphore()
    pl.semaphore_signal(barrier, inc=1, device_id=preceding, device_id_type=pl.DeviceIdType.MESH)

    local_copies = [
        pltpu.make_async_copy(k_hbm, k_buf.at[pl.ds(reach, rows), :], in_sem.at[0]),
        pltpu.make_async_copy(v_hbm, v_buf.at[pl.ds(reach, rows), :], in_sem.at[1]),
        pltpu.make_async_copy(q_hbm, q_buf, in_sem.at[2]),
    ]
    for copy in local_copies:
        copy.start()

    def passing(hop, group):
        columns = pl.ds(group * HEAD_WIDTH, HEAD_WIDTH)
        found = []
        for at, (hbm, buf) in enumerate(((k_hbm, k_buf), (v_hbm, v_buf))):
            if hop == 0:
                source = hbm.at[:, columns]
            else:
                source = buf.at[pl.ds(reach - hop * rows, rows), columns]
            found.append(pltpu.make_async_remote_copy(
                src_ref=source,
                dst_ref=buf.at[pl.ds(reach - (hop + 1) * rows, rows), columns],
                send_sem=send_sem.at[hop, group, at],
                recv_sem=recv_sem.at[hop, group, at],
                device_id=following,
                device_id_type=pl.DeviceIdType.MESH,
            ))
        return found

    copies = [[passing(hop, group) for group in range(key_heads)] for hop in range(hops)]
    pl.semaphore_wait(barrier, 1)
    for group in range(key_heads):
        for copy in copies[0][group]:
            copy.start()

    position = piece * rows + lax.broadcasted_iota(jnp.int32, (rows, LANES), 0)
    starts = document_starts(len_ref[...], position)
    row_at = lax.broadcasted_iota(jnp.int32, (rows, reach), 0)
    column_at = lax.broadcasted_iota(jnp.int32, (rows, reach), 1)
    key_position = piece * rows + column_at - jnp.where(column_at <= row_at, 0, reach)
    bias[...] = jnp.where(key_position >= starts, 0.0, NEG)
    if own_rows > rows:
        k_buf[reach + rows :, :] = jnp.zeros((own_rows - rows, kv_width), k_buf.dtype)
        v_buf[reach + rows :, :] = jnp.zeros((own_rows - rows, kv_width), v_buf.dtype)

    for hop in range(1, hops):
        for group in range(key_heads):
            for before, after in zip(copies[hop - 1][group], copies[hop][group]):
                before.wait_recv()
                after.start()
    for copy in local_copies:
        copy.wait()

    factor = math.log2(math.e) / math.sqrt(HEAD_WIDTH)
    own = lax.broadcasted_iota(jnp.int32, (rows, own_rows), 1) <= lax.broadcasted_iota(
        jnp.int32, (rows, own_rows), 0)
    group_width = QUERY_PER_KEY * HEAD_WIDTH
    written = []
    for group in range(key_heads):
        for copy in copies[hops - 1][group]:
            copy.wait_recv()
        columns = slice(group * HEAD_WIDTH, (group + 1) * HEAD_WIDTH)
        at = [group * group_width + i * HEAD_WIDTH for i in range(QUERY_PER_KEY)]
        stacked = jnp.concatenate([q_buf[:, a : a + HEAD_WIDTH] for a in at], axis=0)
        scores = lax.dot_general(
            stacked, k_buf[:, columns], (((1,), (1,)), ((), ())),
            preferred_element_type=jnp.float32)
        weights, inverses = [], []
        for i in range(QUERY_PER_KEY):
            part = scores[i * rows : (i + 1) * rows]
            first = jnp.where(own, part[:, reach:], part[:, :own_rows]) + bias[:, :own_rows]
            rest = part[:, own_rows:reach] + bias[:, own_rows:]
            top = jnp.maximum(
                jnp.max(first, axis=1, keepdims=True), jnp.max(rest, axis=1, keepdims=True)) * factor
            first = jnp.exp2(first * factor - top)
            rest = jnp.exp2(rest * factor - top)
            total = jnp.sum(first, axis=1, keepdims=True) + jnp.sum(rest, axis=1, keepdims=True)
            inverses.append(1.0 / total)
            weights.append(jnp.concatenate(
                [jnp.where(own, 0.0, first).astype(jnp.bfloat16), rest.astype(jnp.bfloat16),
                 jnp.where(own, first, 0.0).astype(jnp.bfloat16)], axis=1))
        summed = jnp.dot(
            jnp.concatenate(weights, axis=0), v_buf[:, columns],
            preferred_element_type=jnp.float32)
        for i in range(QUERY_PER_KEY):
            o_buf[:, at[i] : at[i] + HEAD_WIDTH] = (
                summed[i * rows : (i + 1) * rows] * inverses[i]).astype(o_buf.dtype)
        span = pl.ds(group * group_width, group_width)
        copy = pltpu.make_async_copy(o_buf.at[:, span], o_hbm.at[:, span], out_sem.at[group])
        copy.start()
        written.append(copy)
    for hop in range(hops):
        for group in range(key_heads):
            for copy in copies[hop][group]:
                copy.wait_send()
    for copy in written:
        copy.wait()


def local(sizes, queries, keys, values, doc_lengths):
    rows, kv_width = keys.shape
    key_heads = kv_width // HEAD_WIDTH
    reach = DOCUMENT_SPAN * rows * sizes[2] // 2
    hops = reach // rows
    own_rows = max(rows, LANES)
    spare = -doc_lengths.shape[0] % (8 * LANES)
    lengths = jnp.pad(doc_lengths, (0, spare)).reshape(-1, LANES)
    anywhere = pl.BlockSpec(memory_space=pl.ANY)
    return pl.pallas_call(
        functools.partial(kernel, sizes),
        out_shape=jax.ShapeDtypeStruct(queries.shape, queries.dtype),
        in_specs=[anywhere, anywhere, anywhere, pl.BlockSpec(memory_space=pltpu.VMEM)],
        out_specs=anywhere,
        scratch_shapes=[
            pltpu.VMEM(queries.shape, queries.dtype),
            pltpu.VMEM((reach + own_rows, kv_width), keys.dtype),
            pltpu.VMEM((reach + own_rows, kv_width), values.dtype),
            pltpu.VMEM(queries.shape, queries.dtype),
            pltpu.VMEM((rows, reach), jnp.float32),
            pltpu.SemaphoreType.DMA((hops, key_heads, 2)),
            pltpu.SemaphoreType.DMA((hops, key_heads, 2)),
            pltpu.SemaphoreType.DMA((3,)),
            pltpu.SemaphoreType.DMA((key_heads,)),
        ],
        compiler_params=pltpu.CompilerParams(
            collective_id=0, has_side_effects=True, vmem_limit_bytes=40 * 1024 * 1024),
        name="ring_attention",
    )(queries, keys, values, lengths)


def solution(mesh):
    sizes = (mesh.shape["outer"], mesh.shape["inner"], mesh.shape["head"])
    spread = P(("outer", "inner", "head"), None)
    return jax.shard_map(
        functools.partial(local, sizes),
        mesh=mesh,
        in_specs=(spread, spread, spread, P()),
        out_specs=spread,
        check_vma=False,
    )
```

```python
import functools
import math

import jax
import jax.numpy as jnp
from jax import lax
from jax.experimental import pallas as pl
from jax.experimental.pallas import tpu as pltpu
from jax.sharding import PartitionSpec as P

HEAD_WIDTH = 128
DOCUMENT_SPAN = 2
QUERY_PER_KEY = 8
LANES = 128

NEG = -1e30


def piece_to_device(piece, contexts, inner_count, per_block):
    block, sub = piece // per_block, piece % per_block
    front = block < contexts
    context = jnp.where(front, block, 2 * contexts - 1 - block)
    head = jnp.where(front, sub, per_block + sub)
    return (context // inner_count, context % inner_count, head)


def document_starts(lengths, positions):
    lane = lax.broadcasted_iota(jnp.int32, lengths.shape, 1)
    within = lengths
    step = 1
    while step < LANES:
        within = within + jnp.where(lane >= step, pltpu.roll(within, step, 1), 0)
        step *= 2
    before = jnp.zeros((1, 1), jnp.int32)
    starts = jnp.zeros(positions.shape, jnp.int32)
    for row in range(lengths.shape[0]):
        ends = before + within[row : row + 1, :]
        starts = jnp.maximum(starts, jnp.where(ends <= positions, ends, 0))
        before = ends[:, LANES - 1 :]
    return jnp.max(starts, axis=1, keepdims=True)


def kernel(sizes, q_hbm, k_hbm, v_hbm, len_hbm, o_buf, q_buf, k_buf, v_buf, len_buf, bias,
           send_sem, recv_sem, in_sem):
    outer_count, inner_count, head_count = sizes
    rows, kv_width = k_hbm.shape
    key_heads = kv_width // HEAD_WIDTH
    contexts = outer_count * inner_count
    per_block = head_count // 2
    reach = DOCUMENT_SPAN * rows * per_block
    hops = reach // rows
    pieces = contexts * head_count
    own_rows = k_buf.shape[0] - reach

    context = lax.axis_index("outer") * inner_count + lax.axis_index("inner")
    head = lax.axis_index("head")
    half, sub = head // per_block, head % per_block
    block = jnp.where(half == 0, context, 2 * contexts - 1 - context)
    piece = block * per_block + sub
    place = functools.partial(
        piece_to_device, contexts=contexts, inner_count=inner_count, per_block=per_block)
    following = place(lax.rem(piece + 1, pieces))
    preceding = place(lax.rem(piece + pieces - 1, pieces))

    barrier = pltpu.get_barrier_semaphore()
    pl.semaphore_signal(barrier, inc=1, device_id=preceding, device_id_type=pl.DeviceIdType.MESH)

    local_copies = [
        pltpu.make_async_copy(len_hbm, len_buf, in_sem.at[0]),
        pltpu.make_async_copy(k_hbm, k_buf.at[pl.ds(reach, rows), :], in_sem.at[1]),
        pltpu.make_async_copy(v_hbm, v_buf.at[pl.ds(reach, rows), :], in_sem.at[2]),
        pltpu.make_async_copy(q_hbm, q_buf, in_sem.at[3]),
    ]
    for copy in local_copies:
        copy.start()

    def passing(hop, group):
        columns = pl.ds(group * HEAD_WIDTH, HEAD_WIDTH)
        found = []
        for at, (hbm, buf) in enumerate(((k_hbm, k_buf), (v_hbm, v_buf))):
            if hop == 0:
                source = hbm.at[:, columns]
            else:
                source = buf.at[pl.ds(reach - hop * rows, rows), columns]
            found.append(pltpu.make_async_remote_copy(
                src_ref=source,
                dst_ref=buf.at[pl.ds(reach - (hop + 1) * rows, rows), columns],
                send_sem=send_sem.at[hop, group, at],
                recv_sem=recv_sem.at[hop, group, at],
                device_id=following,
                device_id_type=pl.DeviceIdType.MESH,
            ))
        return found

    copies = [[passing(hop, group) for group in range(key_heads)] for hop in range(hops)]
    pl.semaphore_wait(barrier, 1)
    for group in range(key_heads):
        for copy in copies[0][group]:
            copy.start()

    position = piece * rows + lax.broadcasted_iota(jnp.int32, (rows, LANES), 0)
    local_copies[0].wait()
    starts = document_starts(len_buf[...], position)
    row_at = lax.broadcasted_iota(jnp.int32, (rows, reach), 0)
    column_at = lax.broadcasted_iota(jnp.int32, (rows, reach), 1)
    key_position = piece * rows + column_at - jnp.where(column_at <= row_at, 0, reach)
    bias[...] = jnp.where(key_position >= starts, 0.0, NEG)
    if own_rows > rows:
        k_buf[reach + rows :, :] = jnp.zeros((own_rows - rows, kv_width), k_buf.dtype)
        v_buf[reach + rows :, :] = jnp.zeros((own_rows - rows, kv_width), v_buf.dtype)

    for hop in range(1, hops):
        for group in range(key_heads):
            for before, after in zip(copies[hop - 1][group], copies[hop][group]):
                before.wait_recv()
                after.start()
    for copy in local_copies[1:]:
        copy.wait()

    factor = math.log2(math.e) / math.sqrt(HEAD_WIDTH)
    own = lax.broadcasted_iota(jnp.int32, (rows, own_rows), 1) <= lax.broadcasted_iota(
        jnp.int32, (rows, own_rows), 0)
    group_width = QUERY_PER_KEY * HEAD_WIDTH
    for group in range(key_heads):
        key_copy, value_copy = copies[hops - 1][group]
        key_copy.wait_recv()
        columns = slice(group * HEAD_WIDTH, (group + 1) * HEAD_WIDTH)
        at = [group * group_width + i * HEAD_WIDTH for i in range(QUERY_PER_KEY)]
        stacked = jnp.concatenate([q_buf[:, a : a + HEAD_WIDTH] for a in at], axis=0)
        scores = lax.dot_general(
            stacked, k_buf[:, columns], (((1,), (1,)), ((), ())),
            preferred_element_type=jnp.float32)
        weights, inverses = [], []
        for i in range(QUERY_PER_KEY):
            part = scores[i * rows : (i + 1) * rows]
            first = jnp.where(own, part[:, reach:], part[:, :own_rows]) + bias[:, :own_rows]
            rest = part[:, own_rows:reach] + bias[:, own_rows:]
            top = jnp.maximum(
                jnp.max(first, axis=1, keepdims=True), jnp.max(rest, axis=1, keepdims=True)) * factor
            first = jnp.exp2(first * factor - top)
            rest = jnp.exp2(rest * factor - top)
            total = jnp.sum(first, axis=1, keepdims=True) + jnp.sum(rest, axis=1, keepdims=True)
            inverses.append(1.0 / total)
            weights.append(jnp.concatenate(
                [jnp.where(own, 0.0, first).astype(jnp.bfloat16), rest.astype(jnp.bfloat16),
                 jnp.where(own, first, 0.0).astype(jnp.bfloat16)], axis=1))
        value_copy.wait_recv()
        summed = jnp.dot(
            jnp.concatenate(weights, axis=0), v_buf[:, columns],
            preferred_element_type=jnp.float32)
        for i in range(QUERY_PER_KEY):
            o_buf[:, at[i] : at[i] + HEAD_WIDTH] = (
                summed[i * rows : (i + 1) * rows] * inverses[i]).astype(o_buf.dtype)
    for hop in range(hops):
        for group in range(key_heads):
            for copy in copies[hop][group]:
                copy.wait_send()


def local(sizes, queries, keys, values, doc_lengths):
    rows, kv_width = keys.shape
    key_heads = kv_width // HEAD_WIDTH
    reach = DOCUMENT_SPAN * rows * sizes[2] // 2
    hops = reach // rows
    own_rows = max(rows, LANES)
    lengths = jnp.pad(doc_lengths, (0, -doc_lengths.shape[0] % LANES)).reshape(-1, LANES)
    operands = [
        pltpu.with_memory_space_constraint(value, pltpu.HBM)
        for value in (queries, keys, values, lengths)
    ]
    in_hbm = pl.BlockSpec(memory_space=pltpu.HBM)
    return pl.pallas_call(
        functools.partial(kernel, sizes),
        out_shape=pltpu.VMEM(queries.shape, queries.dtype),
        in_specs=[in_hbm, in_hbm, in_hbm, in_hbm],
        out_specs=pl.BlockSpec(memory_space=pltpu.VMEM),
        scratch_shapes=[
            pltpu.VMEM(queries.shape, queries.dtype),
            pltpu.VMEM((reach + own_rows, kv_width), keys.dtype),
            pltpu.VMEM((reach + own_rows, kv_width), values.dtype),
            pltpu.VMEM(lengths.shape, lengths.dtype),
            pltpu.VMEM((rows, reach), jnp.float32),
            pltpu.SemaphoreType.DMA((hops, key_heads, 2)),
            pltpu.SemaphoreType.DMA((hops, key_heads, 2)),
            pltpu.SemaphoreType.DMA((4,)),
        ],
        compiler_params=pltpu.CompilerParams(
            collective_id=0, has_side_effects=True, vmem_limit_bytes=40 * 1024 * 1024),
        name="ring_attention",
    )(*operands)


def solution(mesh):
    sizes = (mesh.shape["outer"], mesh.shape["inner"], mesh.shape["head"])
    spread = P(("outer", "inner", "head"), None)
    return jax.shard_map(
        functools.partial(local, sizes),
        mesh=mesh,
        in_specs=(spread, spread, spread, P()),
        out_specs=spread,
        check_vma=False,
    )
```

```python
import functools
import math

import jax
import jax.numpy as jnp
from jax import lax
from jax.experimental import pallas as pl
from jax.experimental.pallas import tpu as pltpu
from jax.sharding import PartitionSpec as P

HEAD_WIDTH = 128
DOCUMENT_SPAN = 2
QUERY_PER_KEY = 8
LANES = 128

NEG = -1e30


def piece_to_device(piece, contexts, inner_count, per_block):
    block, sub = piece // per_block, piece % per_block
    front = block < contexts
    context = jnp.where(front, block, 2 * contexts - 1 - block)
    head = jnp.where(front, sub, per_block + sub)
    return (context // inner_count, context % inner_count, head)


def document_starts(lengths, positions):
    lane = lax.broadcasted_iota(jnp.int32, lengths.shape, 1)
    within = lengths
    step = 1
    while step < LANES:
        within = within + jnp.where(lane >= step, pltpu.roll(within, step, 1), 0)
        step *= 2
    before = jnp.zeros((1, 1), jnp.int32)
    starts = jnp.zeros(positions.shape, jnp.int32)
    for row in range(lengths.shape[0]):
        ends = before + within[row : row + 1, :]
        starts = jnp.maximum(starts, jnp.where(ends <= positions, ends, 0))
        before = ends[:, LANES - 1 :]
    return jnp.max(starts, axis=1, keepdims=True)


def kernel(sizes, q_hbm, k_hbm, v_hbm, len_hbm, o_buf, q_buf, k_buf, v_buf, len_buf, bias,
           send_sem, recv_sem, in_sem):
    outer_count, inner_count, head_count = sizes
    rows, kv_width = k_hbm.shape
    key_heads = kv_width // HEAD_WIDTH
    contexts = outer_count * inner_count
    per_block = head_count // 2
    reach = DOCUMENT_SPAN * rows * per_block
    hops = reach // rows
    pieces = contexts * head_count
    own_rows = k_buf.shape[1] - reach

    context = lax.axis_index("outer") * inner_count + lax.axis_index("inner")
    head = lax.axis_index("head")
    half, sub = head // per_block, head % per_block
    block = jnp.where(half == 0, context, 2 * contexts - 1 - context)
    piece = block * per_block + sub
    place = functools.partial(
        piece_to_device, contexts=contexts, inner_count=inner_count, per_block=per_block)
    following = place(lax.rem(piece + 1, pieces))
    preceding = place(lax.rem(piece + pieces - 1, pieces))

    barrier = pltpu.get_barrier_semaphore()
    pl.semaphore_signal(barrier, inc=1, device_id=preceding, device_id_type=pl.DeviceIdType.MESH)

    own_slot = pl.ds(reach, rows)
    length_copy = pltpu.make_async_copy(len_hbm, len_buf, in_sem.at[0])
    length_copy.start()
    held_copies = []
    for group in range(key_heads):
        columns = pl.ds(group * HEAD_WIDTH, HEAD_WIDTH)
        held_copies.append([
            pltpu.make_async_copy(
                hbm.at[:, columns], buf.at[group, own_slot, :], in_sem.at[2 + 2 * group + at])
            for at, (hbm, buf) in enumerate(((k_hbm, k_buf), (v_hbm, v_buf)))
        ])
        for copy in held_copies[group]:
            copy.start()
    query_copy = pltpu.make_async_copy(q_hbm, q_buf, in_sem.at[1])
    query_copy.start()

    def passing(hop, group):
        return [
            pltpu.make_async_remote_copy(
                src_ref=buf.at[group, pl.ds(reach - hop * rows, rows), :],
                dst_ref=buf.at[group, pl.ds(reach - (hop + 1) * rows, rows), :],
                send_sem=send_sem.at[hop, group, at],
                recv_sem=recv_sem.at[hop, group, at],
                device_id=following,
                device_id_type=pl.DeviceIdType.MESH,
            )
            for at, buf in enumerate((k_buf, v_buf))
        ]

    copies = [[passing(hop, group) for group in range(key_heads)] for hop in range(hops)]

    length_copy.wait()
    position = piece * rows + lax.broadcasted_iota(jnp.int32, (rows, LANES), 0)
    starts = document_starts(len_buf[...], position)
    row_at = lax.broadcasted_iota(jnp.int32, (rows, reach), 0)
    column_at = lax.broadcasted_iota(jnp.int32, (rows, reach), 1)
    key_position = piece * rows + column_at - jnp.where(column_at <= row_at, 0, reach)
    bias[...] = jnp.where(key_position >= starts, 0.0, NEG)
    if own_rows > rows:
        blank = jnp.zeros((key_heads, own_rows - rows, HEAD_WIDTH), k_buf.dtype)
        k_buf[:, reach + rows :, :] = blank
        v_buf[:, reach + rows :, :] = blank
    for pair in held_copies:
        for copy in pair:
            copy.wait()
    pl.semaphore_wait(barrier, 1)

    factor = math.log2(math.e) / math.sqrt(HEAD_WIDTH)
    own = lax.broadcasted_iota(jnp.int32, (rows, own_rows), 1) <= lax.broadcasted_iota(
        jnp.int32, (rows, own_rows), 0)
    group_width = QUERY_PER_KEY * HEAD_WIDTH

    def send(hop, group):
        for at, copy in enumerate(copies[hop][group]):
            if hop > 0:
                copies[hop - 1][group][at].wait_recv()
            copy.start()

    def attend(group):
        if group == 0:
            query_copy.wait()
        at = [group * group_width + i * HEAD_WIDTH for i in range(QUERY_PER_KEY)]
        stacked = jnp.concatenate([q_buf[:, a : a + HEAD_WIDTH] for a in at], axis=0)
        key_copy, value_copy = copies[hops - 1][group]
        key_copy.wait_recv()
        scores = lax.dot_general(
            stacked, k_buf[group], (((1,), (1,)), ((), ())), preferred_element_type=jnp.float32)
        weights, inverses = [], []
        for i in range(QUERY_PER_KEY):
            part = scores[i * rows : (i + 1) * rows]
            first = jnp.where(own, part[:, reach:], part[:, :own_rows]) + bias[:, :own_rows]
            rest = part[:, own_rows:reach] + bias[:, own_rows:]
            top = jnp.max(jnp.maximum(first, rest), axis=1, keepdims=True) * factor
            first = jnp.exp2(first * factor - top)
            rest = jnp.exp2(rest * factor - top)
            inverses.append(1.0 / jnp.sum(first + rest, axis=1, keepdims=True))
            weights.append(jnp.concatenate(
                [jnp.where(own, 0.0, first).astype(jnp.bfloat16), rest.astype(jnp.bfloat16),
                 jnp.where(own, first, 0.0).astype(jnp.bfloat16)], axis=1))
        value_copy.wait_recv()
        summed = jnp.dot(
            jnp.concatenate(weights, axis=0), v_buf[group], preferred_element_type=jnp.float32)
        for i in range(QUERY_PER_KEY):
            o_buf[:, at[i] : at[i] + HEAD_WIDTH] = (
                summed[i * rows : (i + 1) * rows] * inverses[i]).astype(o_buf.dtype)

    events = []
    for group in range(key_heads):
        for hop in range(hops):
            events.append((20 * group + 30 * hop, functools.partial(send, hop, group)))
        events.append((20 * group + 30 * hops + 2, functools.partial(attend, group)))
    for _, event in sorted(events, key=lambda pair: pair[0]):
        event()
    for hop in range(hops):
        for group in range(key_heads):
            for copy in copies[hop][group]:
                copy.wait_send()


def local(sizes, queries, keys, values, doc_lengths):
    rows, kv_width = keys.shape
    key_heads = kv_width // HEAD_WIDTH
    reach = DOCUMENT_SPAN * rows * sizes[2] // 2
    hops = reach // rows
    own_rows = max(rows, LANES)
    lengths = jnp.pad(doc_lengths, (0, -doc_lengths.shape[0] % LANES)).reshape(-1, LANES)
    operands = [
        pltpu.with_memory_space_constraint(value, pltpu.HBM)
        for value in (queries, keys, values, lengths)
    ]
    in_hbm = pl.BlockSpec(memory_space=pltpu.HBM)
    return pl.pallas_call(
        functools.partial(kernel, sizes),
        out_shape=pltpu.VMEM(queries.shape, queries.dtype),
        in_specs=[in_hbm, in_hbm, in_hbm, in_hbm],
        out_specs=pl.BlockSpec(memory_space=pltpu.VMEM),
        scratch_shapes=[
            pltpu.VMEM(queries.shape, queries.dtype),
            pltpu.VMEM((key_heads, reach + own_rows, HEAD_WIDTH), keys.dtype),
            pltpu.VMEM((key_heads, reach + own_rows, HEAD_WIDTH), values.dtype),
            pltpu.VMEM(lengths.shape, lengths.dtype),
            pltpu.VMEM((rows, reach), jnp.float32),
            pltpu.SemaphoreType.DMA((hops, key_heads, 2)),
            pltpu.SemaphoreType.DMA((hops, key_heads, 2)),
            pltpu.SemaphoreType.DMA((2 + 2 * key_heads,)),
        ],
        compiler_params=pltpu.CompilerParams(
            collective_id=0, has_side_effects=True, vmem_limit_bytes=40 * 1024 * 1024),
        name="ring_attention",
    )(*operands)


def solution(mesh):
    sizes = (mesh.shape["outer"], mesh.shape["inner"], mesh.shape["head"])
    spread = P(("outer", "inner", "head"), None)
    return jax.shard_map(
        functools.partial(local, sizes),
        mesh=mesh,
        in_specs=(spread, spread, spread, P()),
        out_specs=spread,
        check_vma=False,
    )
```

```python
import functools
import math

import jax
import jax.numpy as jnp
from jax import lax
from jax.experimental import pallas as pl
from jax.experimental.pallas import tpu as pltpu
from jax.sharding import PartitionSpec as P

HEAD_WIDTH = 128
DOCUMENT_SPAN = 2
QUERY_PER_KEY = 8
LANES = 128

NEG = -1e30


def piece_to_device(piece, contexts, inner_count, per_block):
    block, sub = piece // per_block, piece % per_block
    front = block < contexts
    context = jnp.where(front, block, 2 * contexts - 1 - block)
    head = jnp.where(front, sub, per_block + sub)
    return (context // inner_count, context % inner_count, head)


def document_starts(lengths, positions):
    lane = lax.broadcasted_iota(jnp.int32, lengths.shape, 1)
    within = lengths
    step = 1
    while step < LANES:
        within = within + jnp.where(lane >= step, pltpu.roll(within, step, 1), 0)
        step *= 2
    before = jnp.zeros((1, 1), jnp.int32)
    starts = jnp.zeros(positions.shape, jnp.int32)
    for row in range(lengths.shape[0]):
        ends = before + within[row : row + 1, :]
        starts = jnp.maximum(starts, jnp.where(ends <= positions, ends, 0))
        before = ends[:, LANES - 1 :]
    return jnp.max(starts, axis=1, keepdims=True)


def kernel(sizes, q_hbm, k_hbm, v_hbm, len_hbm, o_buf, q_buf, k_buf, v_buf, len_buf, bias,
           send_sem, recv_sem, in_sem):
    outer_count, inner_count, head_count = sizes
    rows, kv_width = k_hbm.shape
    key_heads = kv_width // HEAD_WIDTH
    contexts = outer_count * inner_count
    per_block = head_count // 2
    reach = DOCUMENT_SPAN * rows * per_block
    hops = reach // rows
    pieces = contexts * head_count
    own_rows = k_buf.shape[1] - reach

    context = lax.axis_index("outer") * inner_count + lax.axis_index("inner")
    head = lax.axis_index("head")
    half, sub = head // per_block, head % per_block
    block = jnp.where(half == 0, context, 2 * contexts - 1 - context)
    piece = block * per_block + sub
    place = functools.partial(
        piece_to_device, contexts=contexts, inner_count=inner_count, per_block=per_block)
    following = place(lax.rem(piece + 1, pieces))
    preceding = place(lax.rem(piece + pieces - 1, pieces))

    paired = hops == 2
    lead = lax.rem(piece, 2) == 0

    barrier = pltpu.get_barrier_semaphore()
    pl.semaphore_signal(barrier, inc=1, device_id=preceding, device_id_type=pl.DeviceIdType.MESH)
    if paired:
        after_next = place(lax.rem(piece + 2, pieces))
        before_last = place(lax.rem(piece + pieces - 2, pieces))

        @pl.when(lead)
        def _():
            pl.semaphore_signal(
                barrier, inc=1, device_id=before_last, device_id_type=pl.DeviceIdType.MESH)

    own_slot = pl.ds(reach, rows)
    length_copy = pltpu.make_async_copy(len_hbm, len_buf, in_sem.at[0])
    length_copy.start()
    held_copies = []
    for group in range(key_heads):
        columns = pl.ds(group * HEAD_WIDTH, HEAD_WIDTH)
        held_copies.append([
            pltpu.make_async_copy(
                hbm.at[:, columns], buf.at[group, own_slot, :], in_sem.at[2 + 2 * group + at])
            for at, (hbm, buf) in enumerate(((k_hbm, k_buf), (v_hbm, v_buf)))
        ])
        for copy in held_copies[group]:
            copy.start()
    query_copy = pltpu.make_async_copy(q_hbm, q_buf, in_sem.at[1])
    query_copy.start()

    def passing(hop, group):
        return [
            pltpu.make_async_remote_copy(
                src_ref=buf.at[group, pl.ds(reach - hop * rows, rows), :],
                dst_ref=buf.at[group, pl.ds(reach - (hop + 1) * rows, rows), :],
                send_sem=send_sem.at[hop, group, at],
                recv_sem=recv_sem.at[hop, group, at],
                device_id=following,
                device_id_type=pl.DeviceIdType.MESH,
            )
            for at, buf in enumerate((k_buf, v_buf))
        ]

    copies = [[passing(hop, group) for group in range(key_heads)] for hop in range(hops)]

    def skipping(group):
        return [
            pltpu.make_async_remote_copy(
                src_ref=buf.at[group, own_slot, :],
                dst_ref=buf.at[group, pl.ds(reach - 2 * rows, rows), :],
                send_sem=send_sem.at[hops, group, at],
                recv_sem=recv_sem.at[1, group, at],
                device_id=after_next,
                device_id_type=pl.DeviceIdType.MESH,
            )
            for at, buf in enumerate((k_buf, v_buf))
        ]

    length_copy.wait()
    position = piece * rows + lax.broadcasted_iota(jnp.int32, (rows, LANES), 0)
    starts = document_starts(len_buf[...], position)
    row_at = lax.broadcasted_iota(jnp.int32, (rows, reach), 0)
    column_at = lax.broadcasted_iota(jnp.int32, (rows, reach), 1)
    key_position = piece * rows + column_at - jnp.where(column_at <= row_at, 0, reach)
    bias[...] = jnp.where(key_position >= starts, 0.0, NEG)
    if own_rows > rows:
        blank = jnp.zeros((key_heads, own_rows - rows, HEAD_WIDTH), k_buf.dtype)
        k_buf[:, reach + rows :, :] = blank
        v_buf[:, reach + rows :, :] = blank
    for pair in held_copies:
        for copy in pair:
            copy.wait()
    pl.semaphore_wait(barrier, jnp.where(lead, 2, 1) if paired else 1)
    if paired:
        @pl.when(lead)
        def _():
            for group in range(key_heads):
                for copy in skipping(group):
                    copy.start()

        for group in range(key_heads):
            for copy in copies[0][group]:
                copy.start()

    factor = math.log2(math.e) / math.sqrt(HEAD_WIDTH)
    own = lax.broadcasted_iota(jnp.int32, (rows, own_rows), 1) <= lax.broadcasted_iota(
        jnp.int32, (rows, own_rows), 0)
    group_width = QUERY_PER_KEY * HEAD_WIDTH

    def send(hop, group):
        for at, copy in enumerate(copies[hop][group]):
            if hop > 0:
                copies[hop - 1][group][at].wait_recv()
            if paired:
                pl.when(lead)(copy.start)
            else:
                copy.start()

    def attend(group):
        if group == 0:
            query_copy.wait()
        at = [group * group_width + i * HEAD_WIDTH for i in range(QUERY_PER_KEY)]
        stacked = jnp.concatenate([q_buf[:, a : a + HEAD_WIDTH] for a in at], axis=0)
        key_copy, value_copy = copies[hops - 1][group]
        key_copy.wait_recv()
        scores = lax.dot_general(
            stacked, k_buf[group], (((1,), (1,)), ((), ())), preferred_element_type=jnp.float32)
        weights, inverses = [], []
        for i in range(QUERY_PER_KEY):
            part = scores[i * rows : (i + 1) * rows]
            first = jnp.where(own, part[:, reach:], part[:, :own_rows]) + bias[:, :own_rows]
            rest = part[:, own_rows:reach] + bias[:, own_rows:]
            top = jnp.max(jnp.maximum(first, rest), axis=1, keepdims=True) * factor
            first = jnp.exp2(first * factor - top)
            rest = jnp.exp2(rest * factor - top)
            inverses.append(1.0 / jnp.sum(first + rest, axis=1, keepdims=True))
            weights.append(jnp.concatenate(
                [jnp.where(own, 0.0, first).astype(jnp.bfloat16), rest.astype(jnp.bfloat16),
                 jnp.where(own, first, 0.0).astype(jnp.bfloat16)], axis=1))
        value_copy.wait_recv()
        summed = jnp.dot(
            jnp.concatenate(weights, axis=0), v_buf[group], preferred_element_type=jnp.float32)
        for i in range(QUERY_PER_KEY):
            o_buf[:, at[i] : at[i] + HEAD_WIDTH] = (
                summed[i * rows : (i + 1) * rows] * inverses[i]).astype(o_buf.dtype)

    events = []
    for group in range(key_heads):
        for hop in range(1 if paired else 0, hops):
            events.append((20 * group + 30 * hop, functools.partial(send, hop, group)))
        events.append((20 * group + 30 * hops + 2, functools.partial(attend, group)))
    for _, event in sorted(events, key=lambda pair: pair[0]):
        event()
    for hop in range(1 if paired else hops):
        for group in range(key_heads):
            for copy in copies[hop][group]:
                copy.wait_send()
    if paired:
        @pl.when(lead)
        def _():
            for group in range(key_heads):
                for copy in copies[1][group] + skipping(group):
                    copy.wait_send()


def local(sizes, queries, keys, values, doc_lengths):
    rows, kv_width = keys.shape
    key_heads = kv_width // HEAD_WIDTH
    reach = DOCUMENT_SPAN * rows * sizes[2] // 2
    hops = reach // rows
    own_rows = max(rows, LANES)
    lengths = jnp.pad(doc_lengths, (0, -doc_lengths.shape[0] % LANES)).reshape(-1, LANES)
    operands = [
        pltpu.with_memory_space_constraint(value, pltpu.HBM)
        for value in (queries, keys, values, lengths)
    ]
    in_hbm = pl.BlockSpec(memory_space=pltpu.HBM)
    return pl.pallas_call(
        functools.partial(kernel, sizes),
        out_shape=pltpu.VMEM(queries.shape, queries.dtype),
        in_specs=[in_hbm, in_hbm, in_hbm, in_hbm],
        out_specs=pl.BlockSpec(memory_space=pltpu.VMEM),
        scratch_shapes=[
            pltpu.VMEM(queries.shape, queries.dtype),
            pltpu.VMEM((key_heads, reach + own_rows, HEAD_WIDTH), keys.dtype),
            pltpu.VMEM((key_heads, reach + own_rows, HEAD_WIDTH), values.dtype),
            pltpu.VMEM(lengths.shape, lengths.dtype),
            pltpu.VMEM((rows, reach), jnp.float32),
            pltpu.SemaphoreType.DMA((hops + 1, key_heads, 2)),
            pltpu.SemaphoreType.DMA((hops, key_heads, 2)),
            pltpu.SemaphoreType.DMA((2 + 2 * key_heads,)),
        ],
        compiler_params=pltpu.CompilerParams(
            collective_id=0, has_side_effects=True, vmem_limit_bytes=40 * 1024 * 1024),
        name="ring_attention",
    )(*operands)


def solution(mesh):
    sizes = (mesh.shape["outer"], mesh.shape["inner"], mesh.shape["head"])
    spread = P(("outer", "inner", "head"), None)
    return jax.shard_map(
        functools.partial(local, sizes),
        mesh=mesh,
        in_specs=(spread, spread, spread, P()),
        out_specs=spread,
        check_vma=False,
    )
```

```python
import functools
import math

import jax
import jax.numpy as jnp
from jax import lax
from jax.experimental import pallas as pl
from jax.experimental.pallas import tpu as pltpu
from jax.sharding import PartitionSpec as P

HEAD_WIDTH = 128
DOCUMENT_SPAN = 2
QUERY_PER_KEY = 8
LANES = 128

NEG = -1e30


def piece_to_device(piece, contexts, inner_count, per_block):
    block, sub = piece // per_block, piece % per_block
    front = block < contexts
    context = jnp.where(front, block, 2 * contexts - 1 - block)
    head = jnp.where(front, sub, per_block + sub)
    return (context // inner_count, context % inner_count, head)


def document_starts(lengths, positions):
    lane = lax.broadcasted_iota(jnp.int32, lengths.shape, 1)
    within = lengths
    step = 1
    while step < LANES:
        within = within + jnp.where(lane >= step, pltpu.roll(within, step, 1), 0)
        step *= 2
    before = jnp.zeros((1, 1), jnp.int32)
    starts = jnp.zeros(positions.shape, jnp.int32)
    for row in range(lengths.shape[0]):
        ends = before + within[row : row + 1, :]
        starts = jnp.maximum(starts, jnp.where(ends <= positions, ends, 0))
        before = ends[:, LANES - 1 :]
    return jnp.max(starts, axis=1, keepdims=True)


def kernel(sizes, q_hbm, k_hbm, v_hbm, len_hbm, o_buf, q_buf, k_buf, v_buf, len_buf, bias,
           send_sem, recv_sem, in_sem):
    outer_count, inner_count, head_count = sizes
    rows, kv_width = k_hbm.shape
    key_heads = kv_width // HEAD_WIDTH
    contexts = outer_count * inner_count
    per_block = head_count // 2
    reach = DOCUMENT_SPAN * rows * per_block
    hops = reach // rows
    pieces = contexts * head_count
    own_rows = k_buf.shape[1] - reach

    context = lax.axis_index("outer") * inner_count + lax.axis_index("inner")
    head = lax.axis_index("head")
    half, sub = head // per_block, head % per_block
    block = jnp.where(half == 0, context, 2 * contexts - 1 - context)
    piece = block * per_block + sub
    place = functools.partial(
        piece_to_device, contexts=contexts, inner_count=inner_count, per_block=per_block)
    following = place(lax.rem(piece + 1, pieces))
    preceding = place(lax.rem(piece + pieces - 1, pieces))

    paired = hops == 2
    lead = lax.rem(piece, 2) == 0

    barrier = pltpu.get_barrier_semaphore()

    def greet(device):
        pl.semaphore_signal(barrier, inc=1, device_id=device, device_id_type=pl.DeviceIdType.MESH)

    has_next = piece + 1 < pieces
    peers = jnp.where(has_next, 1, 0)
    pl.when(piece >= 1)(functools.partial(greet, preceding))
    if paired:
        after_next = place(lax.rem(piece + 2, pieces))
        before_last = place(lax.rem(piece + pieces - 2, pieces))
        has_second = jnp.logical_and(lead, piece + 2 < pieces)
        peers = peers + jnp.where(has_second, 1, 0)
        pl.when(jnp.logical_and(lead, piece >= 2))(functools.partial(greet, before_last))

    own_slot = pl.ds(reach, rows)
    length_copy = pltpu.make_async_copy(len_hbm, len_buf, in_sem.at[0])
    length_copy.start()
    held_copies = []
    for group in range(key_heads):
        columns = pl.ds(group * HEAD_WIDTH, HEAD_WIDTH)
        held_copies.append([
            pltpu.make_async_copy(
                hbm.at[:, columns], buf.at[group, own_slot, :], in_sem.at[2 + 2 * group + at])
            for at, (hbm, buf) in enumerate(((k_hbm, k_buf), (v_hbm, v_buf)))
        ])
        for copy in held_copies[group]:
            copy.start()
    query_copy = pltpu.make_async_copy(q_hbm, q_buf, in_sem.at[1])
    query_copy.start()

    def passing(hop, group):
        return [
            pltpu.make_async_remote_copy(
                src_ref=buf.at[group, pl.ds(reach - hop * rows, rows), :],
                dst_ref=buf.at[group, pl.ds(reach - (hop + 1) * rows, rows), :],
                send_sem=send_sem.at[hop, group, at],
                recv_sem=recv_sem.at[hop, group, at],
                device_id=following,
                device_id_type=pl.DeviceIdType.MESH,
            )
            for at, buf in enumerate((k_buf, v_buf))
        ]

    copies = [[passing(hop, group) for group in range(key_heads)] for hop in range(hops)]

    def skipping(group):
        return [
            pltpu.make_async_remote_copy(
                src_ref=buf.at[group, own_slot, :],
                dst_ref=buf.at[group, pl.ds(reach - 2 * rows, rows), :],
                send_sem=send_sem.at[hops, group, at],
                recv_sem=recv_sem.at[1, group, at],
                device_id=after_next,
                device_id_type=pl.DeviceIdType.MESH,
            )
            for at, buf in enumerate((k_buf, v_buf))
        ]

    length_copy.wait()
    position = piece * rows + lax.broadcasted_iota(jnp.int32, (rows, LANES), 0)
    starts = document_starts(len_buf[...], position)
    row_at = lax.broadcasted_iota(jnp.int32, (rows, reach), 0)
    column_at = lax.broadcasted_iota(jnp.int32, (rows, reach), 1)
    key_position = piece * rows + column_at - jnp.where(column_at <= row_at, 0, reach)
    bias[...] = jnp.where(key_position >= starts, 0.0, NEG)
    if own_rows > rows:
        blank = jnp.zeros((key_heads, own_rows - rows, HEAD_WIDTH), k_buf.dtype)
        k_buf[:, reach + rows :, :] = blank
        v_buf[:, reach + rows :, :] = blank
    for distance in range(1, hops + 1):
        @pl.when(piece < distance)
        def _():
            blank = jnp.zeros((key_heads, rows, HEAD_WIDTH), k_buf.dtype)
            k_buf[:, reach - distance * rows : reach - (distance - 1) * rows, :] = blank
            v_buf[:, reach - distance * rows : reach - (distance - 1) * rows, :] = blank

    for pair in held_copies:
        for copy in pair:
            copy.wait()
    pl.when(has_next)(lambda: pl.semaphore_wait(barrier, peers))

    def start_all(found):
        for copy in found:
            copy.start()

    def wait_sent(found):
        for copy in found:
            copy.wait_send()

    if paired:
        for group in range(key_heads):
            pl.when(has_second)(functools.partial(start_all, skipping(group)))
            pl.when(has_next)(functools.partial(start_all, copies[0][group]))

    factor = math.log2(math.e) / math.sqrt(HEAD_WIDTH)
    own = lax.broadcasted_iota(jnp.int32, (rows, own_rows), 1) <= lax.broadcasted_iota(
        jnp.int32, (rows, own_rows), 0)
    group_width = QUERY_PER_KEY * HEAD_WIDTH

    def sends(hop):
        there = jnp.logical_and(has_next, piece >= hop)
        return jnp.logical_and(there, lead) if paired and hop > 0 else there

    def send(hop, group):
        for at, copy in enumerate(copies[hop][group]):
            if hop > 0:
                pl.when(piece >= hop)(copies[hop - 1][group][at].wait_recv)
            pl.when(sends(hop))(copy.start)

    def columns_of(group):
        return [group * group_width + i * HEAD_WIDTH for i in range(QUERY_PER_KEY)]

    def weigh(group):
        stacked = jnp.concatenate(
            [q_buf[:, a : a + HEAD_WIDTH] for a in columns_of(group)], axis=0)
        scores = lax.dot_general(
            stacked, k_buf[group], (((1,), (1,)), ((), ())), preferred_element_type=jnp.float32)
        weights, inverses = [], []
        for i in range(QUERY_PER_KEY):
            part = scores[i * rows : (i + 1) * rows]
            first = jnp.where(own, part[:, reach:], part[:, :own_rows]) + bias[:, :own_rows]
            rest = part[:, own_rows:reach] + bias[:, own_rows:]
            top = jnp.max(jnp.maximum(first, rest), axis=1, keepdims=True) * factor
            first = jnp.exp2(first * factor - top)
            rest = jnp.exp2(rest * factor - top)
            total = jnp.sum(first + rest, axis=1, keepdims=True)
            estimate = pl.reciprocal(total, approx=True)
            inverses.append(estimate * (2.0 - total * estimate))
            weights.append(jnp.concatenate(
                [jnp.where(own, 0.0, first).astype(jnp.bfloat16), rest.astype(jnp.bfloat16),
                 jnp.where(own, first, 0.0).astype(jnp.bfloat16)], axis=1))
        return jnp.concatenate(weights, axis=0), inverses

    def gather(group, weights, inverses):
        summed = jnp.dot(weights, v_buf[group], preferred_element_type=jnp.float32)
        for i, a in enumerate(columns_of(group)):
            o_buf[:, a : a + HEAD_WIDTH] = (
                summed[i * rows : (i + 1) * rows] * inverses[i]).astype(o_buf.dtype)

    held = []

    def attend(group):
        if group == 0:
            query_copy.wait()
        else:
            pl.when(piece >= hops)(copies[hops - 1][group - 1][1].wait_recv)
        if group < key_heads:
            pl.when(piece >= hops)(copies[hops - 1][group][0].wait_recv)
        if group > 0:
            gather(group - 1, *held.pop())
        if group < key_heads:
            held.append(weigh(group))

    events = []
    for group in range(key_heads + 1):
        if group < key_heads:
            for hop in range(1 if paired else 0, hops):
                events.append((20 * group + 30 * hop, functools.partial(send, hop, group)))
        events.append((20 * group + 30 * hops + 2, functools.partial(attend, group)))
    for _, event in sorted(events, key=lambda pair: pair[0]):
        event()
    for group in range(key_heads):
        for hop in range(hops):
            pl.when(sends(hop))(functools.partial(wait_sent, copies[hop][group]))
        if paired:
            pl.when(has_second)(functools.partial(wait_sent, skipping(group)))


def local(sizes, queries, keys, values, doc_lengths):
    rows, kv_width = keys.shape
    key_heads = kv_width // HEAD_WIDTH
    reach = DOCUMENT_SPAN * rows * sizes[2] // 2
    hops = reach // rows
    own_rows = max(rows, LANES)
    lengths = jnp.pad(doc_lengths, (0, -doc_lengths.shape[0] % LANES)).reshape(-1, LANES)
    operands = [
        pltpu.with_memory_space_constraint(value, pltpu.HBM)
        for value in (queries, keys, values, lengths)
    ]
    in_hbm = pl.BlockSpec(memory_space=pltpu.HBM)
    return pl.pallas_call(
        functools.partial(kernel, sizes),
        out_shape=pltpu.VMEM(queries.shape, queries.dtype),
        in_specs=[in_hbm, in_hbm, in_hbm, in_hbm],
        out_specs=pl.BlockSpec(memory_space=pltpu.VMEM),
        scratch_shapes=[
            pltpu.VMEM(queries.shape, queries.dtype),
            pltpu.VMEM((key_heads, reach + own_rows, HEAD_WIDTH), keys.dtype),
            pltpu.VMEM((key_heads, reach + own_rows, HEAD_WIDTH), values.dtype),
            pltpu.VMEM(lengths.shape, lengths.dtype),
            pltpu.VMEM((rows, reach), jnp.float32),
            pltpu.SemaphoreType.DMA((hops + 1, key_heads, 2)),
            pltpu.SemaphoreType.DMA((hops, key_heads, 2)),
            pltpu.SemaphoreType.DMA((2 + 2 * key_heads,)),
        ],
        compiler_params=pltpu.CompilerParams(
            collective_id=0, has_side_effects=True, vmem_limit_bytes=40 * 1024 * 1024),
        name="ring_attention",
    )(*operands)


def solution(mesh):
    sizes = (mesh.shape["outer"], mesh.shape["inner"], mesh.shape["head"])
    spread = P(("outer", "inner", "head"), None)
    return jax.shard_map(
        functools.partial(local, sizes),
        mesh=mesh,
        in_specs=(spread, spread, spread, P()),
        out_specs=spread,
        check_vma=False,
    )
```

```python
import functools
import math

import jax
import jax.numpy as jnp
from jax import lax
from jax.experimental import pallas as pl
from jax.experimental.pallas import tpu as pltpu
from jax.sharding import PartitionSpec as P

HEAD_WIDTH = 128
DOCUMENT_SPAN = 2
QUERY_PER_KEY = 8
LANES = 128

NEG = -1e30


def piece_to_device(piece, contexts, inner_count, per_block):
    block, sub = piece // per_block, piece % per_block
    front = block < contexts
    context = jnp.where(front, block, 2 * contexts - 1 - block)
    head = jnp.where(front, sub, per_block + sub)
    return (context // inner_count, context % inner_count, head)


def document_starts(lengths, positions):
    lane = lax.broadcasted_iota(jnp.int32, lengths.shape, 1)
    within = lengths
    step = 1
    while step < LANES:
        within = within + jnp.where(lane >= step, pltpu.roll(within, step, 1), 0)
        step *= 2
    before = jnp.zeros((1, 1), jnp.int32)
    starts = jnp.zeros((1, LANES), jnp.float32)
    for row in range(lengths.shape[0]):
        ends = before + within[row : row + 1, :]
        spread = jnp.transpose(
            jnp.broadcast_to(ends.astype(jnp.float32), (LANES, LANES)))
        passed = jnp.where(spread <= positions, spread, 0.0)
        starts = jnp.maximum(starts, jnp.max(passed, axis=0, keepdims=True))
        before = ends[:, LANES - 1 :]
    return starts


def kernel(sizes, q_hbm, k_hbm, v_hbm, len_hbm, o_buf, q_buf, k_buf, v_buf, len_buf, bias,
           send_sem, recv_sem, in_sem):
    outer_count, inner_count, head_count = sizes
    rows, kv_width = k_hbm.shape
    key_heads = kv_width // HEAD_WIDTH
    contexts = outer_count * inner_count
    per_block = head_count // 2
    reach = DOCUMENT_SPAN * rows * per_block
    hops = reach // rows
    pieces = contexts * head_count
    own_rows = k_buf.shape[1] - reach

    context = lax.axis_index("outer") * inner_count + lax.axis_index("inner")
    head = lax.axis_index("head")
    half, sub = head // per_block, head % per_block
    block = jnp.where(half == 0, context, 2 * contexts - 1 - context)
    piece = block * per_block + sub
    place = functools.partial(
        piece_to_device, contexts=contexts, inner_count=inner_count, per_block=per_block)
    following = place(lax.rem(piece + 1, pieces))
    preceding = place(lax.rem(piece + pieces - 1, pieces))

    paired = hops == 2
    lead = lax.rem(piece, 2) == 0

    barrier = pltpu.get_barrier_semaphore()

    def greet(device):
        pl.semaphore_signal(barrier, inc=1, device_id=device, device_id_type=pl.DeviceIdType.MESH)

    has_next = piece + 1 < pieces
    peers = jnp.where(has_next, 1, 0)
    pl.when(piece >= 1)(functools.partial(greet, preceding))
    if paired:
        after_next = place(lax.rem(piece + 2, pieces))
        before_last = place(lax.rem(piece + pieces - 2, pieces))
        has_second = jnp.logical_and(lead, piece + 2 < pieces)
        peers = peers + jnp.where(has_second, 1, 0)
        pl.when(jnp.logical_and(lead, piece >= 2))(functools.partial(greet, before_last))

    own_slot = pl.ds(reach, rows)
    length_copy = pltpu.make_async_copy(len_hbm, len_buf, in_sem.at[0])
    length_copy.start()
    held_copies = []
    for group in range(key_heads):
        columns = pl.ds(group * HEAD_WIDTH, HEAD_WIDTH)
        held_copies.append([
            pltpu.make_async_copy(
                hbm.at[:, columns], buf.at[group, own_slot, :], in_sem.at[2 + 2 * group + at])
            for at, (hbm, buf) in enumerate(((k_hbm, k_buf), (v_hbm, v_buf)))
        ])
        for copy in held_copies[group]:
            copy.start()
    query_copy = pltpu.make_async_copy(q_hbm, q_buf, in_sem.at[1])
    query_copy.start()

    def passing(hop, group):
        return [
            pltpu.make_async_remote_copy(
                src_ref=buf.at[group, pl.ds(reach - hop * rows, rows), :],
                dst_ref=buf.at[group, pl.ds(reach - (hop + 1) * rows, rows), :],
                send_sem=send_sem.at[hop, group, at],
                recv_sem=recv_sem.at[hop, group, at],
                device_id=following,
                device_id_type=pl.DeviceIdType.MESH,
            )
            for at, buf in enumerate((k_buf, v_buf))
        ]

    copies = [[passing(hop, group) for group in range(key_heads)] for hop in range(hops)]

    def skipping(group):
        return [
            pltpu.make_async_remote_copy(
                src_ref=buf.at[group, own_slot, :],
                dst_ref=buf.at[group, pl.ds(reach - 2 * rows, rows), :],
                send_sem=send_sem.at[hops, group, at],
                recv_sem=recv_sem.at[1, group, at],
                device_id=after_next,
                device_id_type=pl.DeviceIdType.MESH,
            )
            for at, buf in enumerate((k_buf, v_buf))
        ]

    length_copy.wait()
    lane_at = lax.rem(lax.broadcasted_iota(jnp.int32, (LANES, LANES), 1), rows)
    starts = document_starts(len_buf[...], (piece * rows + lane_at).astype(jnp.float32))
    key_at = lax.broadcasted_iota(jnp.int32, (reach, LANES), 0)
    query_at = lax.rem(lax.broadcasted_iota(jnp.int32, (reach, LANES), 1), rows)
    key_position = piece * rows + key_at - jnp.where(key_at <= query_at, 0, reach)
    bias[...] = jnp.where(key_position.astype(jnp.float32) >= starts, 0.0, NEG)
    if own_rows > rows:
        blank = jnp.zeros((key_heads, own_rows - rows, HEAD_WIDTH), k_buf.dtype)
        k_buf[:, reach + rows :, :] = blank
        v_buf[:, reach + rows :, :] = blank
    for distance in range(1, hops + 1):
        @pl.when(piece < distance)
        def _():
            blank = jnp.zeros((key_heads, rows, HEAD_WIDTH), k_buf.dtype)
            k_buf[:, reach - distance * rows : reach - (distance - 1) * rows, :] = blank
            v_buf[:, reach - distance * rows : reach - (distance - 1) * rows, :] = blank

    for pair in held_copies:
        for copy in pair:
            copy.wait()
    pl.when(has_next)(lambda: pl.semaphore_wait(barrier, peers))

    def start_all(found):
        for copy in found:
            copy.start()

    def wait_sent(found):
        for copy in found:
            copy.wait_send()

    if paired:
        for group in range(key_heads):
            pl.when(has_second)(functools.partial(start_all, skipping(group)))
            pl.when(has_next)(functools.partial(start_all, copies[0][group]))

    factor = math.log2(math.e) / math.sqrt(HEAD_WIDTH)
    own = lax.broadcasted_iota(jnp.int32, (own_rows, LANES), 0) <= lax.rem(
        lax.broadcasted_iota(jnp.int32, (own_rows, LANES), 1), rows)
    chunks = QUERY_PER_KEY * rows // LANES
    group_width = QUERY_PER_KEY * HEAD_WIDTH

    def sends(hop):
        there = jnp.logical_and(has_next, piece >= hop)
        return jnp.logical_and(there, lead) if paired and hop > 0 else there

    def send(hop, group):
        for at, copy in enumerate(copies[hop][group]):
            if hop > 0:
                pl.when(piece >= hop)(copies[hop - 1][group][at].wait_recv)
            pl.when(sends(hop))(copy.start)

    def columns_of(group):
        return [group * group_width + i * HEAD_WIDTH for i in range(QUERY_PER_KEY)]

    def weigh(group):
        stacked = jnp.concatenate(
            [q_buf[:, a : a + HEAD_WIDTH] for a in columns_of(group)], axis=0)
        scores = lax.dot_general(
            k_buf[group], stacked, (((1,), (1,)), ((), ())), preferred_element_type=jnp.float32)
        weights, inverses = [], []
        for i in range(chunks):
            part = scores[:, i * LANES : (i + 1) * LANES]
            first = jnp.where(own, part[reach:], part[:own_rows]) + bias[:own_rows, :]
            rest = part[own_rows:reach] + bias[own_rows:, :]
            top = jnp.max(jnp.maximum(first, rest), axis=0, keepdims=True) * factor
            first = jnp.exp2(first * factor - top)
            rest = jnp.exp2(rest * factor - top)
            inverses.append(1.0 / jnp.sum(first + rest, axis=0, keepdims=True))
            weights.append(jnp.concatenate(
                [jnp.where(own, 0.0, first).astype(jnp.bfloat16), rest.astype(jnp.bfloat16),
                 jnp.where(own, first, 0.0).astype(jnp.bfloat16)], axis=0))
        return jnp.concatenate(weights, axis=1), inverses

    def gather(group, weights, inverses):
        summed = jnp.dot(
            jnp.transpose(v_buf[group]), weights, preferred_element_type=jnp.float32)
        columns = columns_of(group)
        for i in range(chunks):
            part = summed[:, i * LANES : (i + 1) * LANES] * inverses[i]
            turned = jnp.transpose(part).astype(o_buf.dtype)
            for j in range(LANES // rows):
                a = columns[i * (LANES // rows) + j]
                o_buf[:, a : a + HEAD_WIDTH] = turned[j * rows : (j + 1) * rows]

    held = []

    def attend(group):
        if group == 0:
            query_copy.wait()
        else:
            pl.when(piece >= hops)(copies[hops - 1][group - 1][1].wait_recv)
        if group < key_heads:
            pl.when(piece >= hops)(copies[hops - 1][group][0].wait_recv)
        if group > 0:
            gather(group - 1, *held.pop())
        if group < key_heads:
            held.append(weigh(group))

    events = []
    for group in range(key_heads + 1):
        if group < key_heads:
            for hop in range(1 if paired else 0, hops):
                events.append((20 * group + 30 * hop, functools.partial(send, hop, group)))
        events.append((20 * group + 30 * hops + 2, functools.partial(attend, group)))
    for _, event in sorted(events, key=lambda pair: pair[0]):
        event()
    for group in range(key_heads):
        for hop in range(hops):
            pl.when(sends(hop))(functools.partial(wait_sent, copies[hop][group]))
        if paired:
            pl.when(has_second)(functools.partial(wait_sent, skipping(group)))


def local(sizes, queries, keys, values, doc_lengths):
    rows, kv_width = keys.shape
    key_heads = kv_width // HEAD_WIDTH
    reach = DOCUMENT_SPAN * rows * sizes[2] // 2
    hops = reach // rows
    own_rows = max(rows, LANES)
    lengths = jnp.pad(doc_lengths, (0, -doc_lengths.shape[0] % LANES)).reshape(-1, LANES)
    operands = [
        pltpu.with_memory_space_constraint(value, pltpu.HBM)
        for value in (queries, keys, values, lengths)
    ]
    in_hbm = pl.BlockSpec(memory_space=pltpu.HBM)
    return pl.pallas_call(
        functools.partial(kernel, sizes),
        out_shape=pltpu.VMEM(queries.shape, queries.dtype),
        in_specs=[in_hbm, in_hbm, in_hbm, in_hbm],
        out_specs=pl.BlockSpec(memory_space=pltpu.VMEM),
        scratch_shapes=[
            pltpu.VMEM(queries.shape, queries.dtype),
            pltpu.VMEM((key_heads, reach + own_rows, HEAD_WIDTH), keys.dtype),
            pltpu.VMEM((key_heads, reach + own_rows, HEAD_WIDTH), values.dtype),
            pltpu.VMEM(lengths.shape, lengths.dtype),
            pltpu.VMEM((reach, LANES), jnp.float32),
            pltpu.SemaphoreType.DMA((hops + 1, key_heads, 2)),
            pltpu.SemaphoreType.DMA((hops, key_heads, 2)),
            pltpu.SemaphoreType.DMA((2 + 2 * key_heads,)),
        ],
        compiler_params=pltpu.CompilerParams(
            collective_id=0, has_side_effects=True, vmem_limit_bytes=40 * 1024 * 1024),
        name="ring_attention",
    )(*operands)


def solution(mesh):
    sizes = (mesh.shape["outer"], mesh.shape["inner"], mesh.shape["head"])
    spread = P(("outer", "inner", "head"), None)
    return jax.shard_map(
        functools.partial(local, sizes),
        mesh=mesh,
        in_specs=(spread, spread, spread, P()),
        out_specs=spread,
        check_vma=False,
    )
```

```python
import functools
import math

import jax
import jax.numpy as jnp
from jax import lax
from jax.experimental import pallas as pl
from jax.experimental.pallas import tpu as pltpu
from jax.sharding import PartitionSpec as P

HEAD_WIDTH = 128
DOCUMENT_SPAN = 2
QUERY_PER_KEY = 8
LANES = 128

NEG = -1e30


def piece_to_device(piece, contexts, inner_count, per_block):
    block, sub = piece // per_block, piece % per_block
    front = block < contexts
    context = jnp.where(front, block, 2 * contexts - 1 - block)
    head = jnp.where(front, sub, per_block + sub)
    return (context // inner_count, context % inner_count, head)


def document_starts(lengths, positions):
    lane = lax.broadcasted_iota(jnp.int32, lengths.shape, 1)
    within = lengths
    step = 1
    while step < LANES:
        within = within + jnp.where(lane >= step, pltpu.roll(within, step, 1), 0)
        step *= 2
    before = jnp.zeros((1, 1), jnp.int32)
    starts = jnp.zeros((1, LANES), jnp.float32)
    for row in range(lengths.shape[0]):
        ends = before + within[row : row + 1, :]
        spread = jnp.transpose(
            jnp.broadcast_to(ends.astype(jnp.float32), (LANES, LANES)))
        passed = jnp.where(spread <= positions, spread, 0.0)
        starts = jnp.maximum(starts, jnp.max(passed, axis=0, keepdims=True))
        before = ends[:, LANES - 1 :]
    return starts


def kernel(sizes, q_hbm, k_hbm, v_hbm, len_hbm, o_buf, q_buf, k_buf, v_buf, len_buf, bias,
           send_sem, recv_sem, in_sem):
    outer_count, inner_count, head_count = sizes
    rows, kv_width = k_hbm.shape
    key_heads = kv_width // HEAD_WIDTH
    contexts = outer_count * inner_count
    per_block = head_count // 2
    reach = DOCUMENT_SPAN * rows * per_block
    hops = reach // rows
    pieces = contexts * head_count
    own_rows = k_buf.shape[1] - reach

    context = lax.axis_index("outer") * inner_count + lax.axis_index("inner")
    head = lax.axis_index("head")
    half, sub = head // per_block, head % per_block
    block = jnp.where(half == 0, context, 2 * contexts - 1 - context)
    piece = block * per_block + sub
    place = functools.partial(
        piece_to_device, contexts=contexts, inner_count=inner_count, per_block=per_block)
    following = place(lax.rem(piece + 1, pieces))
    preceding = place(lax.rem(piece + pieces - 1, pieces))

    paired = hops == 2
    lead = lax.rem(piece, 2) == 0

    barrier = pltpu.get_barrier_semaphore()

    def greet(device):
        pl.semaphore_signal(barrier, inc=1, device_id=device, device_id_type=pl.DeviceIdType.MESH)

    has_next = piece + 1 < pieces
    peers = jnp.where(has_next, 1, 0)
    pl.when(piece >= 1)(functools.partial(greet, preceding))
    if paired:
        after_next = place(lax.rem(piece + 2, pieces))
        before_last = place(lax.rem(piece + pieces - 2, pieces))
        has_second = jnp.logical_and(lead, piece + 2 < pieces)
        peers = peers + jnp.where(has_second, 1, 0)
        pl.when(jnp.logical_and(lead, piece >= 2))(functools.partial(greet, before_last))

    own_slot = pl.ds(reach, rows)
    length_copy = pltpu.make_async_copy(len_hbm, len_buf, in_sem.at[0])
    length_copy.start()
    held_copies = []
    for group in range(key_heads):
        columns = pl.ds(group * HEAD_WIDTH, HEAD_WIDTH)
        held_copies.append([
            pltpu.make_async_copy(
                hbm.at[:, columns], buf.at[group, own_slot, :], in_sem.at[2 + 2 * group + at])
            for at, (hbm, buf) in enumerate(((k_hbm, k_buf), (v_hbm, v_buf)))
        ])
        for copy in held_copies[group]:
            copy.start()
    query_copy = pltpu.make_async_copy(q_hbm, q_buf, in_sem.at[1])
    query_copy.start()

    def passing(hop, group):
        return [
            pltpu.make_async_remote_copy(
                src_ref=buf.at[group, pl.ds(reach - hop * rows, rows), :],
                dst_ref=buf.at[group, pl.ds(reach - (hop + 1) * rows, rows), :],
                send_sem=send_sem.at[hop, group, at],
                recv_sem=recv_sem.at[hop, group, at],
                device_id=following,
                device_id_type=pl.DeviceIdType.MESH,
            )
            for at, buf in enumerate((k_buf, v_buf))
        ]

    copies = [[passing(hop, group) for group in range(key_heads)] for hop in range(hops)]

    def skipping(group):
        return [
            pltpu.make_async_remote_copy(
                src_ref=buf.at[group, own_slot, :],
                dst_ref=buf.at[group, pl.ds(reach - 2 * rows, rows), :],
                send_sem=send_sem.at[hops, group, at],
                recv_sem=recv_sem.at[1, group, at],
                device_id=after_next,
                device_id_type=pl.DeviceIdType.MESH,
            )
            for at, buf in enumerate((k_buf, v_buf))
        ]

    length_copy.wait()
    lane_at = lax.rem(lax.broadcasted_iota(jnp.int32, (LANES, LANES), 1), rows)
    starts = document_starts(len_buf[...], (piece * rows + lane_at).astype(jnp.float32))
    key_at = lax.broadcasted_iota(jnp.int32, (reach, LANES), 0)
    query_at = lax.rem(lax.broadcasted_iota(jnp.int32, (reach, LANES), 1), rows)
    key_position = piece * rows + key_at - jnp.where(key_at <= query_at, 0, reach)
    bias[...] = jnp.where(key_position.astype(jnp.float32) >= starts, 0.0, NEG)
    if own_rows > rows:
        blank = jnp.zeros((key_heads, own_rows - rows, HEAD_WIDTH), k_buf.dtype)
        k_buf[:, reach + rows :, :] = blank
        v_buf[:, reach + rows :, :] = blank
    for distance in range(1, hops + 1):
        @pl.when(piece < distance)
        def _():
            blank = jnp.zeros((key_heads, rows, HEAD_WIDTH), k_buf.dtype)
            k_buf[:, reach - distance * rows : reach - (distance - 1) * rows, :] = blank
            v_buf[:, reach - distance * rows : reach - (distance - 1) * rows, :] = blank

    for pair in held_copies:
        for copy in pair:
            copy.wait()
    pl.when(has_next)(lambda: pl.semaphore_wait(barrier, peers))

    def start_all(found):
        for copy in found:
            copy.start()

    def wait_sent(found):
        for copy in found:
            copy.wait_send()

    straight = jnp.logical_and(jnp.logical_not(lead), has_next)

    def start_far(group):
        pl.when(has_second)(functools.partial(start_all, skipping(group)))
        pl.when(straight)(functools.partial(start_all, copies[0][group]))

    def pace(group):
        def swap(done, following_ones):
            for one, other in zip(done, following_ones):
                one.wait_send()
                other.start()

        pl.when(has_second)(functools.partial(swap, skipping(group), skipping(group + 1)))
        pl.when(straight)(functools.partial(swap, copies[0][group], copies[0][group + 1]))

    factor = math.log2(math.e) / math.sqrt(HEAD_WIDTH)
    own = lax.broadcasted_iota(jnp.int32, (own_rows, LANES), 0) <= lax.rem(
        lax.broadcasted_iota(jnp.int32, (own_rows, LANES), 1), rows)
    chunks = QUERY_PER_KEY * rows // LANES
    group_width = QUERY_PER_KEY * HEAD_WIDTH

    def sends(hop):
        there = jnp.logical_and(has_next, piece >= hop)
        return jnp.logical_and(there, lead) if paired and hop > 0 else there

    def send(hop, group):
        for at, copy in enumerate(copies[hop][group]):
            if hop > 0:
                pl.when(piece >= hop)(copies[hop - 1][group][at].wait_recv)
            pl.when(sends(hop))(copy.start)

    def columns_of(group):
        return [group * group_width + i * HEAD_WIDTH for i in range(QUERY_PER_KEY)]

    def weigh(group):
        stacked = jnp.concatenate(
            [q_buf[:, a : a + HEAD_WIDTH] for a in columns_of(group)], axis=0)
        scores = lax.dot_general(
            k_buf[group], stacked, (((1,), (1,)), ((), ())), preferred_element_type=jnp.float32)
        weights, inverses = [], []
        for i in range(chunks):
            part = scores[:, i * LANES : (i + 1) * LANES]
            first = jnp.where(own, part[reach:], part[:own_rows]) + bias[:own_rows, :]
            rest = part[own_rows:reach] + bias[own_rows:, :]
            top = jnp.max(jnp.maximum(first, rest), axis=0, keepdims=True) * factor
            first = jnp.exp2(first * factor - top)
            rest = jnp.exp2(rest * factor - top)
            inverses.append(1.0 / jnp.sum(first + rest, axis=0, keepdims=True))
            weights.append(jnp.concatenate(
                [jnp.where(own, 0.0, first).astype(jnp.bfloat16), rest.astype(jnp.bfloat16),
                 jnp.where(own, first, 0.0).astype(jnp.bfloat16)], axis=0))
        return jnp.concatenate(weights, axis=1), inverses

    def gather(group, weights, inverses):
        summed = jnp.dot(
            jnp.transpose(v_buf[group]), weights, preferred_element_type=jnp.float32)
        columns = columns_of(group)
        for i in range(chunks):
            part = summed[:, i * LANES : (i + 1) * LANES] * inverses[i]
            turned = jnp.transpose(part).astype(o_buf.dtype)
            for j in range(LANES // rows):
                a = columns[i * (LANES // rows) + j]
                o_buf[:, a : a + HEAD_WIDTH] = turned[j * rows : (j + 1) * rows]

    held = []

    def attend(group):
        if group == 0:
            query_copy.wait()
        else:
            pl.when(piece >= hops)(copies[hops - 1][group - 1][1].wait_recv)
        if group < key_heads:
            pl.when(piece >= hops)(copies[hops - 1][group][0].wait_recv)
        if group > 0:
            gather(group - 1, *held.pop())
        if group < key_heads:
            held.append(weigh(group))

    if paired:
        start_far(0)
        for group in range(key_heads):
            pl.when(lead)(functools.partial(start_all, copies[0][group]))
        paced = 0
        for group in range(key_heads):
            if group == 0 and key_heads > 1:
                pace(0)
                paced = 1
            send(1, group)
            if paced < key_heads - 1:
                pace(paced)
                paced += 1
            attend(group)
        attend(key_heads)
        last = key_heads - 1
        pl.when(has_second)(functools.partial(wait_sent, skipping(last)))
        pl.when(straight)(functools.partial(wait_sent, copies[0][last]))
        for group in range(key_heads):
            pl.when(lead)(functools.partial(wait_sent, copies[0][group]))
            pl.when(sends(1))(functools.partial(wait_sent, copies[1][group]))
        return

    events = []
    for group in range(key_heads + 1):
        if group < key_heads:
            for hop in range(hops):
                events.append((20 * group + 30 * hop, functools.partial(send, hop, group)))
        events.append((20 * group + 30 * hops + 2, functools.partial(attend, group)))
    for _, event in sorted(events, key=lambda pair: pair[0]):
        event()
    for group in range(key_heads):
        for hop in range(hops):
            pl.when(sends(hop))(functools.partial(wait_sent, copies[hop][group]))


def local(sizes, queries, keys, values, doc_lengths):
    rows, kv_width = keys.shape
    key_heads = kv_width // HEAD_WIDTH
    reach = DOCUMENT_SPAN * rows * sizes[2] // 2
    hops = reach // rows
    own_rows = max(rows, LANES)
    lengths = jnp.pad(doc_lengths, (0, -doc_lengths.shape[0] % LANES)).reshape(-1, LANES)
    operands = [
        pltpu.with_memory_space_constraint(value, pltpu.HBM)
        for value in (queries, keys, values, lengths)
    ]
    in_hbm = pl.BlockSpec(memory_space=pltpu.HBM)
    return pl.pallas_call(
        functools.partial(kernel, sizes),
        out_shape=pltpu.VMEM(queries.shape, queries.dtype),
        in_specs=[in_hbm, in_hbm, in_hbm, in_hbm],
        out_specs=pl.BlockSpec(memory_space=pltpu.VMEM),
        scratch_shapes=[
            pltpu.VMEM(queries.shape, queries.dtype),
            pltpu.VMEM((key_heads, reach + own_rows, HEAD_WIDTH), keys.dtype),
            pltpu.VMEM((key_heads, reach + own_rows, HEAD_WIDTH), values.dtype),
            pltpu.VMEM(lengths.shape, lengths.dtype),
            pltpu.VMEM((reach, LANES), jnp.float32),
            pltpu.SemaphoreType.DMA((hops + 1, key_heads, 2)),
            pltpu.SemaphoreType.DMA((hops, key_heads, 2)),
            pltpu.SemaphoreType.DMA((2 + 2 * key_heads,)),
        ],
        compiler_params=pltpu.CompilerParams(
            collective_id=0, has_side_effects=True, vmem_limit_bytes=40 * 1024 * 1024),
        name="ring_attention",
    )(*operands)


def solution(mesh):
    sizes = (mesh.shape["outer"], mesh.shape["inner"], mesh.shape["head"])
    spread = P(("outer", "inner", "head"), None)
    return jax.shard_map(
        functools.partial(local, sizes),
        mesh=mesh,
        in_specs=(spread, spread, spread, P()),
        out_specs=spread,
        check_vma=False,
    )
```

```python
import functools
import math

import jax
import jax.numpy as jnp
from jax import lax
from jax.experimental import pallas as pl
from jax.experimental.pallas import tpu as pltpu
from jax.sharding import PartitionSpec as P

HEAD_WIDTH = 128
DOCUMENT_SPAN = 2
QUERY_PER_KEY = 8
LANES = 128

NEG = -1e30


def piece_to_device(piece, contexts, inner_count, per_block):
    block, sub = piece // per_block, piece % per_block
    front = block < contexts
    context = jnp.where(front, block, 2 * contexts - 1 - block)
    head = jnp.where(front, sub, per_block + sub)
    return (context // inner_count, context % inner_count, head)


def document_starts(lengths, positions):
    lane = lax.broadcasted_iota(jnp.int32, lengths.shape, 1)
    within = lengths
    step = 1
    while step < LANES:
        within = within + jnp.where(lane >= step, pltpu.roll(within, step, 1), 0)
        step *= 2
    before = jnp.zeros((1, 1), jnp.int32)
    starts = jnp.zeros((1, LANES), jnp.float32)
    for row in range(lengths.shape[0]):
        ends = before + within[row : row + 1, :]
        spread = jnp.transpose(
            jnp.broadcast_to(ends.astype(jnp.float32), (LANES, LANES)))
        passed = jnp.where(spread <= positions, spread, 0.0)
        starts = jnp.maximum(starts, jnp.max(passed, axis=0, keepdims=True))
        before = ends[:, LANES - 1 :]
    return starts


def weigh_values(values, weights, inverses, out, first_column, rows):
    summed = jnp.dot(jnp.transpose(values), weights, preferred_element_type=jnp.float32)
    per_chunk = LANES // rows
    for i, inverse in enumerate(inverses):
        part = summed[:, i * LANES : (i + 1) * LANES] * inverse
        turned = jnp.transpose(part).astype(out.dtype)
        for j in range(per_chunk):
            a = first_column + (i * per_chunk + j) * HEAD_WIDTH
            out[:, a : a + HEAD_WIDTH] = turned[j * rows : (j + 1) * rows]


def kernel(sizes, q_hbm, k_hbm, v_hbm, len_hbm, o_buf, last_weights, last_inverses, last_values,
           q_buf, k_buf, v_buf, len_buf, bias, send_sem, recv_sem, in_sem):
    outer_count, inner_count, head_count = sizes
    rows, kv_width = k_hbm.shape
    key_heads = kv_width // HEAD_WIDTH
    contexts = outer_count * inner_count
    per_block = head_count // 2
    reach = DOCUMENT_SPAN * rows * per_block
    hops = reach // rows
    pieces = contexts * head_count
    own_rows = k_buf.shape[1] - reach

    context = lax.axis_index("outer") * inner_count + lax.axis_index("inner")
    head = lax.axis_index("head")
    half, sub = head // per_block, head % per_block
    block = jnp.where(half == 0, context, 2 * contexts - 1 - context)
    piece = block * per_block + sub
    place = functools.partial(
        piece_to_device, contexts=contexts, inner_count=inner_count, per_block=per_block)
    following = place(lax.rem(piece + 1, pieces))
    preceding = place(lax.rem(piece + pieces - 1, pieces))

    paired = hops == 2
    lead = lax.rem(piece, 2) == 0

    barrier = pltpu.get_barrier_semaphore()

    def greet(device):
        pl.semaphore_signal(barrier, inc=1, device_id=device, device_id_type=pl.DeviceIdType.MESH)

    has_next = piece + 1 < pieces
    peers = jnp.where(has_next, 1, 0)
    pl.when(piece >= 1)(functools.partial(greet, preceding))
    if paired:
        after_next = place(lax.rem(piece + 2, pieces))
        before_last = place(lax.rem(piece + pieces - 2, pieces))
        has_second = jnp.logical_and(lead, piece + 2 < pieces)
        peers = peers + jnp.where(has_second, 1, 0)
        pl.when(jnp.logical_and(lead, piece >= 2))(functools.partial(greet, before_last))

    own_slot = pl.ds(reach, rows)
    length_copy = pltpu.make_async_copy(len_hbm, len_buf, in_sem.at[0])
    length_copy.start()
    held_copies = []
    for group in range(key_heads):
        columns = pl.ds(group * HEAD_WIDTH, HEAD_WIDTH)
        held_copies.append([
            pltpu.make_async_copy(
                hbm.at[:, columns], buf.at[group, own_slot, :], in_sem.at[2 + 2 * group + at])
            for at, (hbm, buf) in enumerate(((k_hbm, k_buf), (v_hbm, v_buf)))
        ])
        for copy in held_copies[group]:
            copy.start()
    query_copy = pltpu.make_async_copy(q_hbm, q_buf, in_sem.at[1])
    query_copy.start()

    def passing(hop, group):
        return [
            pltpu.make_async_remote_copy(
                src_ref=buf.at[group, pl.ds(reach - hop * rows, rows), :],
                dst_ref=buf.at[group, pl.ds(reach - (hop + 1) * rows, rows), :],
                send_sem=send_sem.at[hop, group, at],
                recv_sem=recv_sem.at[hop, group, at],
                device_id=following,
                device_id_type=pl.DeviceIdType.MESH,
            )
            for at, buf in enumerate((k_buf, v_buf))
        ]

    copies = [[passing(hop, group) for group in range(key_heads)] for hop in range(hops)]

    def skipping(group):
        return [
            pltpu.make_async_remote_copy(
                src_ref=buf.at[group, own_slot, :],
                dst_ref=buf.at[group, pl.ds(reach - 2 * rows, rows), :],
                send_sem=send_sem.at[hops, group, at],
                recv_sem=recv_sem.at[1, group, at],
                device_id=after_next,
                device_id_type=pl.DeviceIdType.MESH,
            )
            for at, buf in enumerate((k_buf, v_buf))
        ]

    length_copy.wait()
    lane_at = lax.rem(lax.broadcasted_iota(jnp.int32, (LANES, LANES), 1), rows)
    starts = document_starts(len_buf[...], (piece * rows + lane_at).astype(jnp.float32))
    key_at = lax.broadcasted_iota(jnp.int32, (reach, LANES), 0)
    query_at = lax.rem(lax.broadcasted_iota(jnp.int32, (reach, LANES), 1), rows)
    key_position = piece * rows + key_at - jnp.where(key_at <= query_at, 0, reach)
    bias[...] = jnp.where(key_position.astype(jnp.float32) >= starts, 0.0, NEG)
    if own_rows > rows:
        blank = jnp.zeros((key_heads, own_rows - rows, HEAD_WIDTH), k_buf.dtype)
        k_buf[:, reach + rows :, :] = blank
        v_buf[:, reach + rows :, :] = blank
    for distance in range(1, hops + 1):
        @pl.when(piece < distance)
        def _():
            blank = jnp.zeros((key_heads, rows, HEAD_WIDTH), k_buf.dtype)
            k_buf[:, reach - distance * rows : reach - (distance - 1) * rows, :] = blank
            v_buf[:, reach - distance * rows : reach - (distance - 1) * rows, :] = blank

    for pair in held_copies:
        for copy in pair:
            copy.wait()
    pl.when(has_next)(lambda: pl.semaphore_wait(barrier, peers))

    def start_all(found):
        for copy in found:
            copy.start()

    def wait_sent(found):
        for copy in found:
            copy.wait_send()

    if paired:
        for group in range(key_heads):
            pl.when(has_second)(functools.partial(start_all, skipping(group)))
            pl.when(has_next)(functools.partial(start_all, copies[0][group]))

    factor = math.log2(math.e) / math.sqrt(HEAD_WIDTH)
    own = lax.broadcasted_iota(jnp.int32, (own_rows, LANES), 0) <= lax.rem(
        lax.broadcasted_iota(jnp.int32, (own_rows, LANES), 1), rows)
    chunks = QUERY_PER_KEY * rows // LANES
    group_width = QUERY_PER_KEY * HEAD_WIDTH

    def sends(hop):
        there = jnp.logical_and(has_next, piece >= hop)
        return jnp.logical_and(there, lead) if paired and hop > 0 else there

    def send(hop, group):
        for at, copy in enumerate(copies[hop][group]):
            if hop > 0:
                pl.when(piece >= hop)(copies[hop - 1][group][at].wait_recv)
            pl.when(sends(hop))(copy.start)

    def columns_of(group):
        return [group * group_width + i * HEAD_WIDTH for i in range(QUERY_PER_KEY)]

    def weigh(group):
        stacked = jnp.concatenate(
            [q_buf[:, a : a + HEAD_WIDTH] for a in columns_of(group)], axis=0)
        scores = lax.dot_general(
            k_buf[group], stacked, (((1,), (1,)), ((), ())), preferred_element_type=jnp.float32)
        weights, inverses = [], []
        for i in range(chunks):
            part = scores[:, i * LANES : (i + 1) * LANES]
            first = jnp.where(own, part[reach:], part[:own_rows]) + bias[:own_rows, :]
            rest = part[own_rows:reach] + bias[own_rows:, :]
            top = jnp.max(jnp.maximum(first, rest), axis=0, keepdims=True) * factor
            first = jnp.exp2(first * factor - top)
            rest = jnp.exp2(rest * factor - top)
            inverses.append(1.0 / jnp.sum(first + rest, axis=0, keepdims=True))
            weights.append(jnp.concatenate(
                [jnp.where(own, 0.0, first).astype(jnp.bfloat16), rest.astype(jnp.bfloat16),
                 jnp.where(own, first, 0.0).astype(jnp.bfloat16)], axis=0))
        return jnp.concatenate(weights, axis=1), inverses

    def gather(group, weights, inverses):
        if group < key_heads - 1:
            weigh_values(v_buf[group], weights, inverses, o_buf, group * group_width, rows)
            return
        last_weights[...] = weights
        last_values[...] = v_buf[group]
        for i, inverse in enumerate(inverses):
            last_inverses[i : i + 1, :] = inverse

    held = []

    def attend(group):
        if group == 0:
            query_copy.wait()
        else:
            pl.when(piece >= hops)(copies[hops - 1][group - 1][1].wait_recv)
        if group < key_heads:
            pl.when(piece >= hops)(copies[hops - 1][group][0].wait_recv)
        if group > 0:
            gather(group - 1, *held.pop())
        if group < key_heads:
            held.append(weigh(group))

    events = []
    for group in range(key_heads + 1):
        if group < key_heads:
            for hop in range(1 if paired else 0, hops):
                events.append((20 * group + 30 * hop, functools.partial(send, hop, group)))
        events.append((20 * group + 30 * hops + 2, functools.partial(attend, group)))
    for _, event in sorted(events, key=lambda pair: pair[0]):
        event()
    for group in range(key_heads):
        for hop in range(hops):
            pl.when(sends(hop))(functools.partial(wait_sent, copies[hop][group]))
        if paired:
            pl.when(has_second)(functools.partial(wait_sent, skipping(group)))


def finish(early, weights, inverses, values, o_hbm, late, sems):
    rows, width = early.shape
    early_copy = pltpu.make_async_copy(early, o_hbm.at[:, pl.ds(0, width)], sems.at[0])
    early_copy.start()
    parts = [inverses[i : i + 1, :] for i in range(inverses.shape[0])]
    weigh_values(values[...], weights[...], parts, late, 0, rows)
    late_copy = pltpu.make_async_copy(late, o_hbm.at[:, pl.ds(width, late.shape[1])], sems.at[1])
    late_copy.start()
    early_copy.wait()
    late_copy.wait()


def local(sizes, queries, keys, values, doc_lengths):
    rows, kv_width = keys.shape
    key_heads = kv_width // HEAD_WIDTH
    reach = DOCUMENT_SPAN * rows * sizes[2] // 2
    hops = reach // rows
    own_rows = max(rows, LANES)
    lengths = jnp.pad(doc_lengths, (0, -doc_lengths.shape[0] % LANES)).reshape(-1, LANES)
    operands = [
        pltpu.with_memory_space_constraint(value, pltpu.HBM)
        for value in (queries, keys, values, lengths)
    ]
    in_hbm = pl.BlockSpec(memory_space=pltpu.HBM)
    group_width = QUERY_PER_KEY * HEAD_WIDTH
    early_width = (key_heads - 1) * group_width
    chunks = QUERY_PER_KEY * rows // LANES
    in_vmem = pl.BlockSpec(memory_space=pltpu.VMEM)
    found = pl.pallas_call(
        functools.partial(kernel, sizes),
        out_shape=[
            pltpu.VMEM((rows, early_width), queries.dtype),
            pltpu.VMEM((reach + own_rows, chunks * LANES), jnp.bfloat16),
            pltpu.VMEM((chunks, LANES), jnp.float32),
            pltpu.VMEM((reach + own_rows, HEAD_WIDTH), values.dtype),
        ],
        in_specs=[in_hbm, in_hbm, in_hbm, in_hbm],
        out_specs=[in_vmem] * 4,
        scratch_shapes=[
            pltpu.VMEM(queries.shape, queries.dtype),
            pltpu.VMEM((key_heads, reach + own_rows, HEAD_WIDTH), keys.dtype),
            pltpu.VMEM((key_heads, reach + own_rows, HEAD_WIDTH), values.dtype),
            pltpu.VMEM(lengths.shape, lengths.dtype),
            pltpu.VMEM((reach, LANES), jnp.float32),
            pltpu.SemaphoreType.DMA((hops + 1, key_heads, 2)),
            pltpu.SemaphoreType.DMA((hops, key_heads, 2)),
            pltpu.SemaphoreType.DMA((2 + 2 * key_heads,)),
        ],
        compiler_params=pltpu.CompilerParams(
            collective_id=0, has_side_effects=True, vmem_limit_bytes=40 * 1024 * 1024),
        name="ring_attention",
    )(*operands)
    return pl.pallas_call(
        finish,
        out_shape=jax.ShapeDtypeStruct(queries.shape, queries.dtype),
        in_specs=[in_vmem] * 4,
        out_specs=in_hbm,
        scratch_shapes=[
            pltpu.VMEM((rows, group_width), queries.dtype),
            pltpu.SemaphoreType.DMA((2,)),
        ],
        compiler_params=pltpu.CompilerParams(vmem_limit_bytes=16 * 1024 * 1024),
        name="write_result",
    )(*[pltpu.with_memory_space_constraint(value, pltpu.VMEM) for value in found])


def solution(mesh):
    sizes = (mesh.shape["outer"], mesh.shape["inner"], mesh.shape["head"])
    spread = P(("outer", "inner", "head"), None)
    return jax.shard_map(
        functools.partial(local, sizes),
        mesh=mesh,
        in_specs=(spread, spread, spread, P()),
        out_specs=spread,
        check_vma=False,
    )
```

```python
import functools
import math

import jax
import jax.numpy as jnp
from jax import lax
from jax.experimental import pallas as pl
from jax.experimental.pallas import tpu as pltpu
from jax.sharding import PartitionSpec as P

HEAD_WIDTH = 128
DOCUMENT_SPAN = 2
QUERY_PER_KEY = 8
LANES = 128

NEG = -1e30


def piece_to_device(piece, contexts, inner_count, per_block):
    block, sub = piece // per_block, piece % per_block
    front = block < contexts
    context = jnp.where(front, block, 2 * contexts - 1 - block)
    head = jnp.where(front, sub, per_block + sub)
    return (context // inner_count, context % inner_count, head)


def document_starts(lengths, positions):
    lane = lax.broadcasted_iota(jnp.int32, lengths.shape, 1)
    within = lengths
    step = 1
    while step < LANES:
        within = within + jnp.where(lane >= step, pltpu.roll(within, step, 1), 0)
        step *= 2
    before = jnp.zeros((1, 1), jnp.int32)
    starts = jnp.zeros((1, LANES), jnp.float32)
    for row in range(lengths.shape[0]):
        ends = before + within[row : row + 1, :]
        spread = jnp.transpose(
            jnp.broadcast_to(ends.astype(jnp.float32), (LANES, LANES)))
        passed = jnp.where(spread <= positions, spread, 0.0)
        starts = jnp.maximum(starts, jnp.max(passed, axis=0, keepdims=True))
        before = ends[:, LANES - 1 :]
    return starts


def weigh_values(values, weights, inverses, out, first_column, rows):
    summed = jnp.dot(jnp.transpose(values), weights, preferred_element_type=jnp.float32)
    per_chunk = LANES // rows
    for i, inverse in enumerate(inverses):
        part = summed[:, i * LANES : (i + 1) * LANES] * inverse
        turned = jnp.transpose(part.astype(out.dtype))
        for j in range(per_chunk):
            a = first_column + (i * per_chunk + j) * HEAD_WIDTH
            out[:, a : a + HEAD_WIDTH] = turned[j * rows : (j + 1) * rows]


def kernel(sizes, q_hbm, k_hbm, v_hbm, len_hbm, o_buf, last_weights, last_inverses, last_values,
           q_buf, k_buf, v_buf, len_buf, bias, send_sem, recv_sem, in_sem):
    outer_count, inner_count, head_count = sizes
    rows, kv_width = k_hbm.shape
    key_heads = kv_width // HEAD_WIDTH
    contexts = outer_count * inner_count
    per_block = head_count // 2
    reach = DOCUMENT_SPAN * rows * per_block
    hops = reach // rows
    pieces = contexts * head_count
    own_rows = k_buf.shape[1] - reach

    context = lax.axis_index("outer") * inner_count + lax.axis_index("inner")
    head = lax.axis_index("head")
    half, sub = head // per_block, head % per_block
    block = jnp.where(half == 0, context, 2 * contexts - 1 - context)
    piece = block * per_block + sub
    place = functools.partial(
        piece_to_device, contexts=contexts, inner_count=inner_count, per_block=per_block)
    following = place(lax.rem(piece + 1, pieces))
    preceding = place(lax.rem(piece + pieces - 1, pieces))

    paired = hops == 2
    lead = lax.rem(piece, 2) == 0

    barrier = pltpu.get_barrier_semaphore()

    def greet(device):
        pl.semaphore_signal(barrier, inc=1, device_id=device, device_id_type=pl.DeviceIdType.MESH)

    has_next = piece + 1 < pieces
    peers = jnp.where(has_next, 1, 0)
    pl.when(piece >= 1)(functools.partial(greet, preceding))
    if paired:
        after_next = place(lax.rem(piece + 2, pieces))
        before_last = place(lax.rem(piece + pieces - 2, pieces))
        has_second = jnp.logical_and(lead, piece + 2 < pieces)
        peers = peers + jnp.where(has_second, 1, 0)
        pl.when(jnp.logical_and(lead, piece >= 2))(functools.partial(greet, before_last))

    own_slot = pl.ds(reach, rows)
    length_copy = pltpu.make_async_copy(len_hbm, len_buf, in_sem.at[0])
    length_copy.start()
    held_copies = []
    for group in range(key_heads):
        columns = pl.ds(group * HEAD_WIDTH, HEAD_WIDTH)
        held_copies.append([
            pltpu.make_async_copy(
                hbm.at[:, columns], buf.at[group, own_slot, :], in_sem.at[2 + 2 * group + at])
            for at, (hbm, buf) in enumerate(((k_hbm, k_buf), (v_hbm, v_buf)))
        ])
        for copy in held_copies[group]:
            copy.start()
    query_copy = pltpu.make_async_copy(q_hbm, q_buf, in_sem.at[1])
    query_copy.start()

    def passing(hop, group):
        return [
            pltpu.make_async_remote_copy(
                src_ref=buf.at[group, pl.ds(reach - hop * rows, rows), :],
                dst_ref=buf.at[group, pl.ds(reach - (hop + 1) * rows, rows), :],
                send_sem=send_sem.at[hop, group, at],
                recv_sem=recv_sem.at[hop, group, at],
                device_id=following,
                device_id_type=pl.DeviceIdType.MESH,
            )
            for at, buf in enumerate((k_buf, v_buf))
        ]

    copies = [[passing(hop, group) for group in range(key_heads)] for hop in range(hops)]

    def skipping(group):
        return [
            pltpu.make_async_remote_copy(
                src_ref=buf.at[group, own_slot, :],
                dst_ref=buf.at[group, pl.ds(reach - 2 * rows, rows), :],
                send_sem=send_sem.at[hops, group, at],
                recv_sem=recv_sem.at[1, group, at],
                device_id=after_next,
                device_id_type=pl.DeviceIdType.MESH,
            )
            for at, buf in enumerate((k_buf, v_buf))
        ]

    length_copy.wait()
    lane_at = lax.rem(lax.broadcasted_iota(jnp.int32, (LANES, LANES), 1), rows)
    starts = document_starts(len_buf[...], (piece * rows + lane_at).astype(jnp.float32))
    key_at = lax.broadcasted_iota(jnp.int32, (reach, LANES), 0)
    query_at = lax.rem(lax.broadcasted_iota(jnp.int32, (reach, LANES), 1), rows)
    key_position = piece * rows + key_at - jnp.where(key_at <= query_at, 0, reach)
    bias[...] = jnp.where(key_position.astype(jnp.float32) >= starts, 0.0, NEG)
    if own_rows > rows:
        blank = jnp.zeros((key_heads, own_rows - rows, HEAD_WIDTH), k_buf.dtype)
        k_buf[:, reach + rows :, :] = blank
        v_buf[:, reach + rows :, :] = blank
    for distance in range(1, hops + 1):
        @pl.when(piece < distance)
        def _():
            blank = jnp.zeros((key_heads, rows, HEAD_WIDTH), k_buf.dtype)
            k_buf[:, reach - distance * rows : reach - (distance - 1) * rows, :] = blank
            v_buf[:, reach - distance * rows : reach - (distance - 1) * rows, :] = blank

    for pair in held_copies:
        for copy in pair:
            copy.wait()
    pl.when(has_next)(lambda: pl.semaphore_wait(barrier, peers))

    def start_all(found):
        for copy in found:
            copy.start()

    def wait_sent(found):
        for copy in found:
            copy.wait_send()

    straight = jnp.logical_and(jnp.logical_not(lead), has_next)
    ahead = min(2, key_heads)

    def swap(done, later):
        for one, other in zip(done, later):
            one.wait_send()
            other.start()

    def pace(group):
        later = group + ahead
        if later < key_heads:
            pl.when(has_second)(functools.partial(swap, skipping(group), skipping(later)))
            pl.when(straight)(functools.partial(swap, copies[0][group], copies[0][later]))

    if paired:
        for group in range(ahead):
            pl.when(has_second)(functools.partial(start_all, skipping(group)))
            pl.when(straight)(functools.partial(start_all, copies[0][group]))
        for group in range(key_heads):
            pl.when(lead)(functools.partial(start_all, copies[0][group]))

    factor = math.log2(math.e) / math.sqrt(HEAD_WIDTH)
    own = lax.broadcasted_iota(jnp.int32, (own_rows, LANES), 0) <= lax.rem(
        lax.broadcasted_iota(jnp.int32, (own_rows, LANES), 1), rows)
    chunks = QUERY_PER_KEY * rows // LANES
    group_width = QUERY_PER_KEY * HEAD_WIDTH

    def sends(hop):
        there = jnp.logical_and(has_next, piece >= hop)
        return jnp.logical_and(there, lead) if paired and hop > 0 else there

    def send(hop, group):
        if paired:
            pace(group)
        for at, copy in enumerate(copies[hop][group]):
            if hop > 0:
                pl.when(piece >= hop)(copies[hop - 1][group][at].wait_recv)
            pl.when(sends(hop))(copy.start)

    def columns_of(group):
        return [group * group_width + i * HEAD_WIDTH for i in range(QUERY_PER_KEY)]

    def weigh(group):
        stacked = jnp.concatenate(
            [q_buf[:, a : a + HEAD_WIDTH] for a in columns_of(group)], axis=0)
        scores = lax.dot_general(
            k_buf[group], stacked, (((1,), (1,)), ((), ())), preferred_element_type=jnp.float32)
        weights, inverses = [], []
        for i in range(chunks):
            part = scores[:, i * LANES : (i + 1) * LANES]
            first = jnp.where(own, part[reach:], part[:own_rows]) + bias[:own_rows, :]
            rest = part[own_rows:reach] + bias[own_rows:, :]
            top = jnp.max(jnp.maximum(first, rest), axis=0, keepdims=True) * factor
            first = jnp.exp2(first * factor - top)
            rest = jnp.exp2(rest * factor - top)
            inverses.append(1.0 / jnp.sum(first + rest, axis=0, keepdims=True))
            weights.append(jnp.concatenate(
                [jnp.where(own, 0.0, first).astype(jnp.bfloat16), rest.astype(jnp.bfloat16),
                 jnp.where(own, first, 0.0).astype(jnp.bfloat16)], axis=0))
        return jnp.concatenate(weights, axis=1), inverses

    def gather(group, weights, inverses):
        if group < key_heads - 1:
            weigh_values(v_buf[group], weights, inverses, o_buf, group * group_width, rows)
            return
        last_weights[...] = weights
        last_values[...] = v_buf[group]
        for i, inverse in enumerate(inverses):
            last_inverses[i : i + 1, :] = inverse

    held = []

    def attend(group):
        if group == 0:
            query_copy.wait()
        else:
            pl.when(piece >= hops)(copies[hops - 1][group - 1][1].wait_recv)
        if group < key_heads:
            pl.when(piece >= hops)(copies[hops - 1][group][0].wait_recv)
        if group > 0:
            gather(group - 1, *held.pop())
        if group < key_heads:
            held.append(weigh(group))

    events = []
    for group in range(key_heads + 1):
        if group < key_heads:
            for hop in range(1 if paired else 0, hops):
                events.append((20 * group + 30 * hop, functools.partial(send, hop, group)))
        events.append((20 * group + 30 * hops + 2, functools.partial(attend, group)))
    for _, event in sorted(events, key=lambda pair: pair[0]):
        event()
    for group in range(key_heads):
        for hop in range(hops):
            if paired and hop == 0:
                pl.when(lead)(functools.partial(wait_sent, copies[0][group]))
                if group + ahead >= key_heads:
                    pl.when(has_second)(functools.partial(wait_sent, skipping(group)))
                    pl.when(straight)(functools.partial(wait_sent, copies[0][group]))
            else:
                pl.when(sends(hop))(functools.partial(wait_sent, copies[hop][group]))


def finish(early, weights, inverses, values, o_hbm, late, sems):
    rows, width = early.shape
    early_copy = pltpu.make_async_copy(early, o_hbm.at[:, pl.ds(0, width)], sems.at[0])
    early_copy.start()
    parts = [inverses[i : i + 1, :] for i in range(inverses.shape[0])]
    weigh_values(values[...], weights[...], parts, late, 0, rows)
    late_copy = pltpu.make_async_copy(late, o_hbm.at[:, pl.ds(width, late.shape[1])], sems.at[1])
    late_copy.start()
    early_copy.wait()
    late_copy.wait()


def local(sizes, queries, keys, values, doc_lengths):
    rows, kv_width = keys.shape
    key_heads = kv_width // HEAD_WIDTH
    reach = DOCUMENT_SPAN * rows * sizes[2] // 2
    hops = reach // rows
    own_rows = max(rows, LANES)
    lengths = jnp.pad(doc_lengths, (0, -doc_lengths.shape[0] % LANES)).reshape(-1, LANES)
    operands = [
        pltpu.with_memory_space_constraint(value, pltpu.HBM)
        for value in (queries, keys, values, lengths)
    ]
    in_hbm = pl.BlockSpec(memory_space=pltpu.HBM)
    group_width = QUERY_PER_KEY * HEAD_WIDTH
    early_width = (key_heads - 1) * group_width
    chunks = QUERY_PER_KEY * rows // LANES
    in_vmem = pl.BlockSpec(memory_space=pltpu.VMEM)
    found = pl.pallas_call(
        functools.partial(kernel, sizes),
        out_shape=[
            pltpu.VMEM((rows, early_width), queries.dtype),
            pltpu.VMEM((reach + own_rows, chunks * LANES), jnp.bfloat16),
            pltpu.VMEM((chunks, LANES), jnp.float32),
            pltpu.VMEM((reach + own_rows, HEAD_WIDTH), values.dtype),
        ],
        in_specs=[in_hbm, in_hbm, in_hbm, in_hbm],
        out_specs=[in_vmem] * 4,
        scratch_shapes=[
            pltpu.VMEM(queries.shape, queries.dtype),
            pltpu.VMEM((key_heads, reach + own_rows, HEAD_WIDTH), keys.dtype),
            pltpu.VMEM((key_heads, reach + own_rows, HEAD_WIDTH), values.dtype),
            pltpu.VMEM(lengths.shape, lengths.dtype),
            pltpu.VMEM((reach, LANES), jnp.float32),
            pltpu.SemaphoreType.DMA((hops + 1, key_heads, 2)),
            pltpu.SemaphoreType.DMA((hops, key_heads, 2)),
            pltpu.SemaphoreType.DMA((2 + 2 * key_heads,)),
        ],
        compiler_params=pltpu.CompilerParams(
            collective_id=0, has_side_effects=True, vmem_limit_bytes=40 * 1024 * 1024),
        name="ring_attention",
    )(*operands)
    return pl.pallas_call(
        finish,
        out_shape=jax.ShapeDtypeStruct(queries.shape, queries.dtype),
        in_specs=[in_vmem] * 4,
        out_specs=in_hbm,
        scratch_shapes=[
            pltpu.VMEM((rows, group_width), queries.dtype),
            pltpu.SemaphoreType.DMA((2,)),
        ],
        compiler_params=pltpu.CompilerParams(vmem_limit_bytes=16 * 1024 * 1024),
        name="write_result",
    )(*[pltpu.with_memory_space_constraint(value, pltpu.VMEM) for value in found])


def solution(mesh):
    sizes = (mesh.shape["outer"], mesh.shape["inner"], mesh.shape["head"])
    spread = P(("outer", "inner", "head"), None)
    return jax.shard_map(
        functools.partial(local, sizes),
        mesh=mesh,
        in_specs=(spread, spread, spread, P()),
        out_specs=spread,
        check_vma=False,
    )
```

```python
import functools
import math

import jax
import jax.numpy as jnp
from jax import lax
from jax.experimental import pallas as pl
from jax.experimental.pallas import tpu as pltpu
from jax.sharding import PartitionSpec as P

HEAD_WIDTH = 128
DOCUMENT_SPAN = 2
QUERY_PER_KEY = 8
LANES = 128

NEG = -1e30


def piece_to_device(piece, contexts, inner_count, per_block):
    block, sub = piece // per_block, piece % per_block
    front = block < contexts
    context = jnp.where(front, block, 2 * contexts - 1 - block)
    head = jnp.where(front, sub, per_block + sub)
    return (context // inner_count, context % inner_count, head)


def document_starts(lengths, positions):
    lane = lax.broadcasted_iota(jnp.int32, lengths.shape, 1)
    within = lengths
    step = 1
    while step < LANES:
        within = within + jnp.where(lane >= step, pltpu.roll(within, step, 1), 0)
        step *= 2
    before = jnp.zeros((1, 1), jnp.int32)
    starts = jnp.zeros((1, LANES), jnp.float32)
    for row in range(lengths.shape[0]):
        ends = before + within[row : row + 1, :]
        spread = jnp.transpose(
            jnp.broadcast_to(ends.astype(jnp.float32), (LANES, LANES)))
        passed = jnp.where(spread <= positions, spread, 0.0)
        starts = jnp.maximum(starts, jnp.max(passed, axis=0, keepdims=True))
        before = ends[:, LANES - 1 :]
    return starts


def weigh_values(values, weights, inverses, out, first_column, rows):
    summed = jnp.dot(jnp.transpose(values), weights, preferred_element_type=jnp.float32)
    per_chunk = LANES // rows
    for i, inverse in enumerate(inverses):
        part = summed[:, i * LANES : (i + 1) * LANES] * inverse
        turned = jnp.transpose(part.astype(out.dtype))
        for j in range(per_chunk):
            a = first_column + (i * per_chunk + j) * HEAD_WIDTH
            out[:, a : a + HEAD_WIDTH] = turned[j * rows : (j + 1) * rows]


def kernel(sizes, q_hbm, k_hbm, v_hbm, len_hbm, o_buf, last_weights, last_inverses, last_values,
           q_buf, k_buf, v_buf, len_buf, bias, send_sem, recv_sem, in_sem):
    outer_count, inner_count, head_count = sizes
    rows, kv_width = k_hbm.shape
    key_heads = kv_width // HEAD_WIDTH
    contexts = outer_count * inner_count
    per_block = head_count // 2
    reach = DOCUMENT_SPAN * rows * per_block
    hops = reach // rows
    pieces = contexts * head_count
    own_rows = k_buf.shape[1] - reach

    context = lax.axis_index("outer") * inner_count + lax.axis_index("inner")
    head = lax.axis_index("head")
    half, sub = head // per_block, head % per_block
    block = jnp.where(half == 0, context, 2 * contexts - 1 - context)
    piece = block * per_block + sub
    place = functools.partial(
        piece_to_device, contexts=contexts, inner_count=inner_count, per_block=per_block)
    following = place(lax.rem(piece + 1, pieces))
    preceding = place(lax.rem(piece + pieces - 1, pieces))

    paired = hops == 2
    lead = lax.rem(piece, 2) == 0

    barrier = pltpu.get_barrier_semaphore()

    def greet(device):
        pl.semaphore_signal(barrier, inc=1, device_id=device, device_id_type=pl.DeviceIdType.MESH)

    has_next = piece + 1 < pieces
    peers = jnp.where(has_next, 1, 0)
    pl.when(piece >= 1)(functools.partial(greet, preceding))
    if paired:
        after_next = place(lax.rem(piece + 2, pieces))
        before_last = place(lax.rem(piece + pieces - 2, pieces))
        has_second = jnp.logical_and(lead, piece + 2 < pieces)
        peers = peers + jnp.where(has_second, 1, 0)
        pl.when(jnp.logical_and(lead, piece >= 2))(functools.partial(greet, before_last))

    own_slot = pl.ds(reach, rows)
    length_copy = pltpu.make_async_copy(len_hbm, len_buf, in_sem.at[0])
    length_copy.start()
    held_copies = []
    for group in range(key_heads):
        columns = pl.ds(group * HEAD_WIDTH, HEAD_WIDTH)
        held_copies.append([
            pltpu.make_async_copy(
                hbm.at[:, columns], buf.at[group, own_slot, :], in_sem.at[2 + 2 * group + at])
            for at, (hbm, buf) in enumerate(((k_hbm, k_buf), (v_hbm, v_buf)))
        ])
        for copy in held_copies[group]:
            copy.start()
    query_copy = pltpu.make_async_copy(q_hbm, q_buf, in_sem.at[1])
    query_copy.start()

    def passing(hop, group):
        return [
            pltpu.make_async_remote_copy(
                src_ref=buf.at[group, pl.ds(reach - hop * rows, rows), :],
                dst_ref=buf.at[group, pl.ds(reach - (hop + 1) * rows, rows), :],
                send_sem=send_sem.at[hop, group, at],
                recv_sem=recv_sem.at[hop, group, at],
                device_id=following,
                device_id_type=pl.DeviceIdType.MESH,
            )
            for at, buf in enumerate((k_buf, v_buf))
        ]

    copies = [[passing(hop, group) for group in range(key_heads)] for hop in range(hops)]

    def skipping(group):
        return [
            pltpu.make_async_remote_copy(
                src_ref=buf.at[group, own_slot, :],
                dst_ref=buf.at[group, pl.ds(reach - 2 * rows, rows), :],
                send_sem=send_sem.at[hops, group, at],
                recv_sem=recv_sem.at[1, group, at],
                device_id=after_next,
                device_id_type=pl.DeviceIdType.MESH,
            )
            for at, buf in enumerate((k_buf, v_buf))
        ]

    length_copy.wait()
    lane_at = lax.rem(lax.broadcasted_iota(jnp.int32, (LANES, LANES), 1), rows)
    starts = document_starts(len_buf[...], (piece * rows + lane_at).astype(jnp.float32))
    key_at = lax.broadcasted_iota(jnp.int32, (reach, LANES), 0)
    query_at = lax.rem(lax.broadcasted_iota(jnp.int32, (reach, LANES), 1), rows)
    key_position = piece * rows + key_at - jnp.where(key_at <= query_at, 0, reach)
    bias[...] = jnp.where(key_position.astype(jnp.float32) >= starts, 0.0, NEG)
    if own_rows > rows:
        blank = jnp.zeros((key_heads, own_rows - rows, HEAD_WIDTH), k_buf.dtype)
        k_buf[:, reach + rows :, :] = blank
        v_buf[:, reach + rows :, :] = blank
    for distance in range(1, hops + 1):
        @pl.when(piece < distance)
        def _():
            blank = jnp.zeros((key_heads, rows, HEAD_WIDTH), k_buf.dtype)
            k_buf[:, reach - distance * rows : reach - (distance - 1) * rows, :] = blank
            v_buf[:, reach - distance * rows : reach - (distance - 1) * rows, :] = blank

    for pair in held_copies:
        for copy in pair:
            copy.wait()
    pl.when(has_next)(lambda: pl.semaphore_wait(barrier, peers))

    def start_all(found):
        for copy in found:
            copy.start()

    def wait_sent(found):
        for copy in found:
            copy.wait_send()

    straight = jnp.logical_and(jnp.logical_not(lead), has_next)
    ahead = min(2, key_heads)

    def swap(done, later):
        for one, other in zip(done, later):
            one.wait_send()
            other.start()

    def pace(group):
        later = group + ahead
        if later < key_heads:
            pl.when(has_second)(functools.partial(swap, skipping(group), skipping(later)))
            pl.when(straight)(functools.partial(swap, copies[0][group], copies[0][later]))

    if paired:
        for group in range(ahead):
            pl.when(has_second)(functools.partial(start_all, skipping(group)))
            pl.when(straight)(functools.partial(start_all, copies[0][group]))
        for group in range(key_heads):
            pl.when(lead)(functools.partial(start_all, copies[0][group]))

    factor = math.log2(math.e) / math.sqrt(HEAD_WIDTH)
    own = lax.broadcasted_iota(jnp.int32, (own_rows, LANES), 0) <= lax.rem(
        lax.broadcasted_iota(jnp.int32, (own_rows, LANES), 1), rows)
    own_mask = jnp.where(own, 1.0, 0.0).astype(jnp.bfloat16)
    chunks = QUERY_PER_KEY * rows // LANES
    group_width = QUERY_PER_KEY * HEAD_WIDTH

    def sends(hop):
        there = jnp.logical_and(has_next, piece >= hop)
        return jnp.logical_and(there, lead) if paired and hop > 0 else there

    def send(hop, group):
        if paired:
            pace(group)
        for at, copy in enumerate(copies[hop][group]):
            if hop > 0:
                pl.when(piece >= hop)(copies[hop - 1][group][at].wait_recv)
            pl.when(sends(hop))(copy.start)

    def columns_of(group):
        return [group * group_width + i * HEAD_WIDTH for i in range(QUERY_PER_KEY)]

    def weigh(group):
        stacked = jnp.concatenate(
            [q_buf[:, a : a + HEAD_WIDTH] for a in columns_of(group)], axis=0)
        scores = lax.dot_general(
            k_buf[group], stacked, (((1,), (1,)), ((), ())), preferred_element_type=jnp.float32)
        weights, inverses = [], []
        for i in range(chunks):
            part = scores[:, i * LANES : (i + 1) * LANES]
            first = jnp.where(own, part[reach:], part[:own_rows]) + bias[:own_rows, :]
            rest = part[own_rows:reach] + bias[own_rows:, :]
            top = jnp.max(jnp.maximum(first, rest), axis=0, keepdims=True) * factor
            first = jnp.exp2(first * factor - top)
            rest = jnp.exp2(rest * factor - top)
            inverses.append(1.0 / jnp.sum(first + rest, axis=0, keepdims=True))
            rounded = first.astype(jnp.bfloat16)
            near = rounded * own_mask
            weights.append(jnp.concatenate(
                [rounded - near, rest.astype(jnp.bfloat16), near], axis=0))
        return jnp.concatenate(weights, axis=1), inverses

    def gather(group, weights, inverses):
        if group < key_heads - 1:
            weigh_values(v_buf[group], weights, inverses, o_buf, group * group_width, rows)
            return
        last_weights[...] = weights
        last_values[...] = v_buf[group]
        for i, inverse in enumerate(inverses):
            last_inverses[i : i + 1, :] = inverse

    held = []

    def attend(group):
        if group == 0:
            query_copy.wait()
        else:
            pl.when(piece >= hops)(copies[hops - 1][group - 1][1].wait_recv)
        if group < key_heads:
            pl.when(piece >= hops)(copies[hops - 1][group][0].wait_recv)
        if group > 0:
            gather(group - 1, *held.pop())
        if group < key_heads:
            held.append(weigh(group))

    events = []
    for group in range(key_heads + 1):
        if group < key_heads:
            for hop in range(1 if paired else 0, hops):
                events.append((20 * group + 30 * hop, functools.partial(send, hop, group)))
        events.append((20 * group + 30 * hops + 2, functools.partial(attend, group)))
    for _, event in sorted(events, key=lambda pair: pair[0]):
        event()
    for group in range(key_heads):
        for hop in range(hops):
            if paired and hop == 0:
                pl.when(lead)(functools.partial(wait_sent, copies[0][group]))
                if group + ahead >= key_heads:
                    pl.when(has_second)(functools.partial(wait_sent, skipping(group)))
                    pl.when(straight)(functools.partial(wait_sent, copies[0][group]))
            else:
                pl.when(sends(hop))(functools.partial(wait_sent, copies[hop][group]))


def finish(early, weights, inverses, values, o_hbm, late, sems):
    rows, width = early.shape
    early_copy = pltpu.make_async_copy(early, o_hbm.at[:, pl.ds(0, width)], sems.at[0])
    early_copy.start()
    parts = [inverses[i : i + 1, :] for i in range(inverses.shape[0])]
    half = late.shape[1] // 2
    per_half = len(parts) // 2
    late_copies = []
    for i in range(2):
        lanes = slice(i * per_half * LANES, (i + 1) * per_half * LANES)
        weigh_values(
            values[...], weights[:, lanes], parts[i * per_half : (i + 1) * per_half],
            late, i * half, rows)
        late_copies.append(pltpu.make_async_copy(
            late.at[:, pl.ds(i * half, half)], o_hbm.at[:, pl.ds(width + i * half, half)],
            sems.at[1 + i]))
        late_copies[i].start()
    early_copy.wait()
    for copy in late_copies:
        copy.wait()


def local(sizes, queries, keys, values, doc_lengths):
    rows, kv_width = keys.shape
    key_heads = kv_width // HEAD_WIDTH
    reach = DOCUMENT_SPAN * rows * sizes[2] // 2
    hops = reach // rows
    own_rows = max(rows, LANES)
    lengths = jnp.pad(doc_lengths, (0, -doc_lengths.shape[0] % LANES)).reshape(-1, LANES)
    operands = [
        pltpu.with_memory_space_constraint(value, pltpu.HBM)
        for value in (queries, keys, values, lengths)
    ]
    in_hbm = pl.BlockSpec(memory_space=pltpu.HBM)
    group_width = QUERY_PER_KEY * HEAD_WIDTH
    early_width = (key_heads - 1) * group_width
    chunks = QUERY_PER_KEY * rows // LANES
    in_vmem = pl.BlockSpec(memory_space=pltpu.VMEM)
    found = pl.pallas_call(
        functools.partial(kernel, sizes),
        out_shape=[
            pltpu.VMEM((rows, early_width), queries.dtype),
            pltpu.VMEM((reach + own_rows, chunks * LANES), jnp.bfloat16),
            pltpu.VMEM((chunks, LANES), jnp.float32),
            pltpu.VMEM((reach + own_rows, HEAD_WIDTH), values.dtype),
        ],
        in_specs=[in_hbm, in_hbm, in_hbm, in_hbm],
        out_specs=[in_vmem] * 4,
        scratch_shapes=[
            pltpu.VMEM(queries.shape, queries.dtype),
            pltpu.VMEM((key_heads, reach + own_rows, HEAD_WIDTH), keys.dtype),
            pltpu.VMEM((key_heads, reach + own_rows, HEAD_WIDTH), values.dtype),
            pltpu.VMEM(lengths.shape, lengths.dtype),
            pltpu.VMEM((reach, LANES), jnp.float32),
            pltpu.SemaphoreType.DMA((hops + 1, key_heads, 2)),
            pltpu.SemaphoreType.DMA((hops, key_heads, 2)),
            pltpu.SemaphoreType.DMA((2 + 2 * key_heads,)),
        ],
        compiler_params=pltpu.CompilerParams(
            collective_id=0, has_side_effects=True, vmem_limit_bytes=40 * 1024 * 1024),
        name="ring_attention",
    )(*operands)
    return pl.pallas_call(
        finish,
        out_shape=jax.ShapeDtypeStruct(queries.shape, queries.dtype),
        in_specs=[in_vmem] * 4,
        out_specs=in_hbm,
        scratch_shapes=[
            pltpu.VMEM((rows, group_width), queries.dtype),
            pltpu.SemaphoreType.DMA((3,)),
        ],
        compiler_params=pltpu.CompilerParams(vmem_limit_bytes=16 * 1024 * 1024),
        name="write_result",
    )(*[pltpu.with_memory_space_constraint(value, pltpu.VMEM) for value in found])


def solution(mesh):
    sizes = (mesh.shape["outer"], mesh.shape["inner"], mesh.shape["head"])
    spread = P(("outer", "inner", "head"), None)
    return jax.shard_map(
        functools.partial(local, sizes),
        mesh=mesh,
        in_specs=(spread, spread, spread, P()),
        out_specs=spread,
        check_vma=False,
    )
```
